512 devices in a mesh: dp: 16 (over z, core), tm: 32 (over y, x).
Axes of the slice: x: 4, y: 8, z: 8, core: 2. Of those that a mesh axis runs over, the one named last changes fastest.
Arguments:
- frames_in: bfloat16 [16, 96, 32, 8, 320], P('dp', 'tm'), may hold values from -6 to 6
- cotangent: bfloat16 [16, 96, 32, 8, 320], P('dp', 'tm'), may hold values from -6 to 6
- counts: int32 [16, 32], P('dp'), may hold values from 1 to 3, 64 in all within a row
- norm_gain: float32 [320], replicated, may hold values from 0.5 to 1.5
- norm_shift: float32 [320], replicated, may hold values from -3 to 3
- spatial_weight: bfloat16 [2880, 320], replicated, may hold values from -0.109375 to 0.109375
- temporal_weight: bfloat16 [960, 320], replicated, may hold values from -0.1875 to 0.1875
Outputs:
- input_grad: bfloat16 [16, 96, 32, 8, 320], P('dp', 'tm')
- temporal_grad: float32 [960, 320], replicated
The draws below stay inside these ranges and needn't reach their ends.
Inputs may be any that keep to these rules, and one draw needn't show every extreme that they name: `counts`: each row sums to 64; in every row some index of tm holds exactly 3 frames.
All inputs are finite; a program needn't handle non-finite values.
Results may differ from the reference program's by a relative error of at most 0.006.
Values may be sent and summed in bfloat16 or wider, within the bound.
No kernel may reach another device: no remote copies, remote signals or barrier semaphores. Data moves between devices by JAX's collectives and lax.ppermute only.
A program may use at most 64 MiB of HBM per device.

```python
import math
import jax
import jax.numpy as jnp
import numpy as np
from jax import lax

C = 320
GROUPS = 32
CAP = 3
WW = 8
HH = 32
FRAMES = 64
SLOTS = 96
VIDEOS = 16
N_TM = 32


def spiked(array, own_key, source, target, parts, factor):
    owner, partner = [(jnp.arange(array.shape[axis_at]) // (array.shape[axis_at] // parts)).reshape([-1 if axis == axis_at else 1 for axis in range(array.ndim)]) for axis_at in (source, target)]
    chosen = jax.random.permutation(own_key, parts)[partner]
    strong = (owner == chosen) | (owner == (partner + parts // 2) % parts)
    return jnp.where(strong, factor * array, array)


def block_levels(own_key, shape, cuts, least, top_value):
    def one(axis_at, shards_of):
        steps = jax.random.uniform(jax.random.fold_in(jax.random.fold_in(own_key, 6), axis_at), (shards_of,), jnp.float32, least / len(cuts), top_value / len(cuts))
        return jnp.repeat(jnp.exp(steps), shape[axis_at] // shards_of).reshape((-1,) + (1,) * (len(shape) - axis_at - 1))

    level = one(*cuts[0])
    for cut in cuts[1:]:
        level = level * one(*cut)
    return level


def profile(amount, total, reach, lean):
    weights = [(1 << 20) // math.isqrt(standing ** lean) + 1 for standing in range(2, amount + 1)]
    spare, given = total - reach - (amount - 1), [1] * (amount - 1)
    while spare > 0:
        free = [i for i in range(amount - 1) if given[i] < reach]
        mass, left = sum([weights[i] for i in free]), spare
        for i in free:
            extra = min(reach - given[i], max(1, left * weights[i] // mass), spare)
            given[i] = given[i] + extra
            spare = spare - extra
    return np.array([reach] + given)


def uneven_parts(rng, count, total, most, skew):
    if count == 2:
        one = jax.random.randint(rng, (), max(1, total - most), min(most, total - 1) + 1)
        return jnp.stack([one, total - one])
    sizes = jnp.asarray(profile(count, total, most, skew), jnp.int32)
    couples = (count - 1) // 2
    donor, receiver = sizes[1:1 + 2 * couples:2], sizes[2:2 + 2 * couples:2]
    slack = jnp.minimum(donor - 1, most - receiver)
    shifted = jax.random.randint(jax.random.fold_in(rng, 1), (couples,), 0, 1 << 20) % (slack + 1)
    sizes = sizes.at[1:1 + 2 * couples:2].set(donor - shifted).at[2:2 + 2 * couples:2].set(receiver + shifted)
    return sizes[jax.random.permutation(jax.random.fold_in(rng, 2), count)]


def gaussian(key, shape, scale, bound, split=(), held_as=jnp.bfloat16):
    values = scale * jax.random.normal(key, shape, jnp.float32)
    if split:
        values = values * block_levels(key, shape, split, -0.22, 0.18)
    return jnp.clip(values, -bound, bound).astype(held_as)


def noise_with(own_key, extent, scale, most, split, heavy, kind=jnp.bfloat16):
    values = scale * jax.random.normal(own_key, extent, jnp.float32)
    if split:
        values = values * block_levels(own_key, extent, split, -0.22, 0.18)
    return jnp.clip(spiked(values, jax.random.fold_in(own_key, 3), *heavy), -most, most).astype(kind)


def setup_inputs(seed: int = 0) -> dict:
    streams_of = jax.random.split(jax.random.key(seed), 8)
    return {
        "frames_in": gaussian(streams_of[0], (VIDEOS, SLOTS, HH, WW, C), 1.0, 6.0, ((0, 16), (1, 32))),
        "cotangent": noise_with(streams_of[1], (VIDEOS, SLOTS, HH, WW, C), 1.0, 6.0, ((0, 16), (1, 32)), (1, 4, 32, 2.75)),
        "counts": jax.vmap(lambda own: uneven_parts(own, N_TM, FRAMES, CAP, 0))(jax.random.split(streams_of[2], VIDEOS)).reshape((VIDEOS, N_TM)).astype(jnp.int32),
        "norm_gain": jnp.clip(1.0 + 0.1 * jax.random.normal(streams_of[3], (C,), jnp.float32), 0.5, 1.5),
        "norm_shift": gaussian(streams_of[4], (C,), 0.5, 3.0, (), jnp.float32),
        "spatial_weight": gaussian(streams_of[5], (9 * C, C), (9 * C) ** -0.5, 0.109375),
        "temporal_weight": gaussian(streams_of[6], (3 * C, C), (3 * C) ** -0.5, 0.1875),
    }


def norm_act(values, gain, shift, groups):
    nframes, height, width, channels = values.shape
    per_group = channels // groups
    entries = height * width * per_group

    def group_mean(totals):
        summed = totals.reshape(nframes, groups, per_group).sum(axis=2) / entries
        return jnp.repeat(summed, per_group, axis=1).reshape(nframes, 1, 1, channels)
    centre = group_mean(values.sum(axis=(1, 2)))
    centred = values - centre
    spread = group_mean((centred * centred).sum(axis=(1, 2)))
    normed = centred * lax.rsqrt(spread + 1e-05) * gain + shift
    return jax.nn.silu(normed)

def patches(field):
    height, width = (field.shape[1], field.shape[2])
    padded = jnp.pad(field, ((0, 0), (1, 1), (1, 1), (0, 0)))
    pieces = [padded[:, row_off:row_off + height, col_off:col_off + width, :] for row_off in range(3) for col_off in range(3)]
    return jnp.concatenate(pieces, axis=3)

def spatial_conv(field, weight):
    stacked = patches(field)
    leading = stacked.shape[:3]
    product = jnp.dot(stacked.reshape(-1, stacked.shape[3]), weight, preferred_element_type=jnp.float32)
    return product.reshape(leading + (weight.shape[1],))

def spatial_conv_t(field, weight):
    channels = weight.shape[1]
    flipped = weight.reshape(9, -1, channels)[::-1].transpose(0, 2, 1).reshape(-1, weight.shape[0] // 9)
    return spatial_conv(field, flipped)

def silu_grad(values):
    sigma = jax.nn.sigmoid(values)
    return sigma * (1.0 + values * (1.0 - sigma))

def temporal_core(y_ext, g_ext, weight):
    nframes = y_ext.shape[0] - 2
    channels = weight.shape[1]
    units = jax.nn.silu(y_ext.astype(jnp.float32)).astype(jnp.bfloat16)
    g_mid = g_ext[1:-1].reshape(-1, channels)
    grads = []
    back_sum = jnp.zeros((g_mid.shape[0], channels), jnp.float32)
    for tap_k in range(3):
        taken = units[tap_k:tap_k + nframes].reshape(-1, channels)
        grads.append(lax.dot_general(taken, g_mid, (((0,), (0,)), ((), ())), preferred_element_type=jnp.float32))
        tap_weight = weight[tap_k * channels:(tap_k + 1) * channels]
        source = g_ext[2 - tap_k:2 - tap_k + nframes].reshape(-1, channels)
        back_sum = back_sum + lax.dot_general(source, tap_weight, (((1,), (1,)), ((), ())), preferred_element_type=jnp.float32)
    middle = y_ext[1:-1]
    back_t = (silu_grad(middle.astype(jnp.float32)) * back_sum.reshape(middle.shape)).astype(jnp.bfloat16)
    return (back_t, jnp.concatenate(grads, axis=0))

def frame_slots(counts_row, nframes, cap):
    ndevices = counts_row.shape[0]
    ends = jnp.cumsum(counts_row).astype(jnp.int32)
    starts = ends - counts_row
    frame_ids = jnp.arange(nframes, dtype=jnp.int32)
    owner = lax.optimization_barrier(jnp.sum((ends[None, :] <= frame_ids[:, None]).astype(jnp.int32), axis=1))
    device_ids = jnp.arange(ndevices, dtype=jnp.int32)
    first = lax.optimization_barrier(jnp.sum(jnp.where(device_ids[None, :] == owner[:, None], starts[None, :], 0), axis=1))
    return (owner * cap + frame_ids - first).astype(jnp.int32)

def slot_frames(counts_row, cap):
    ndevices = counts_row.shape[0]
    ends = jnp.cumsum(counts_row).astype(jnp.int32)
    starts = ends - counts_row
    slot_ids = jnp.arange(ndevices * cap, dtype=jnp.int32)
    device = slot_ids // cap
    inner = slot_ids % cap
    device_ids = jnp.arange(ndevices, dtype=jnp.int32)
    onehot = device[:, None] == device_ids[None, :]
    held = lax.optimization_barrier(jnp.sum(jnp.where(onehot, counts_row[None, :], 0), axis=1))
    first = lax.optimization_barrier(jnp.sum(jnp.where(onehot, starts[None, :], 0), axis=1))
    live = inner < held
    return (jnp.where(live, first + inner, 0).astype(jnp.int32), live)

def reference(frames_in, cotangent, counts, norm_gain, norm_shift, spatial_weight, temporal_weight):

    def one_video(members):
        slot_inputs, slot_cotan, counts_row = members
        pick = frame_slots(counts_row, FRAMES, CAP)
        inputs = jnp.take(slot_inputs, pick, axis=0)
        cotan = jnp.take(slot_cotan, pick, axis=0)

        def activate(values):
            return norm_act(values, norm_gain, norm_shift, GROUPS)
        inputs_f = inputs.astype(jnp.float32)
        act_f, act_back = jax.vjp(activate, inputs_f)
        acts = act_f.astype(jnp.bfloat16)
        mixed = spatial_conv(acts, spatial_weight)
        y_out = (inputs_f + mixed).astype(jnp.bfloat16)
        pad_spec = ((1, 1), (0, 0), (0, 0), (0, 0))
        back_t, grad_part = temporal_core(jnp.pad(y_out, pad_spec), jnp.pad(cotan, pad_spec), temporal_weight)
        d_out = (cotan.astype(jnp.float32) + back_t.astype(jnp.float32)).astype(jnp.bfloat16)
        d_act = spatial_conv_t(d_out, spatial_weight)
        d_in = (d_out.astype(jnp.float32) + act_back(d_act)[0]).astype(jnp.bfloat16)
        back_idx, live = slot_frames(counts_row, CAP)
        d_slots = jnp.where(live[:, None, None, None], jnp.take(d_in, back_idx, axis=0), jnp.zeros((), jnp.bfloat16))
        return (d_slots.astype(jnp.bfloat16), grad_part)
    input_grad, grads = lax.map(one_video, (frames_in, cotangent, counts))
    scale = 1.0 / math.sqrt(VIDEOS * FRAMES * HH * WW)
    temporal_grad = lax.optimization_barrier(jnp.sum(grads, axis=0)) * scale
    return (input_grad, temporal_grad)
```

```python
import math

import jax
import jax.numpy as jnp
from jax import lax
from jax.experimental import pallas as pl
from jax.experimental.pallas import tpu as pltpu
from jax.sharding import Mesh
from jax.sharding import PartitionSpec as P

F32 = jnp.float32
BF16 = jnp.bfloat16
C = 320
GROUPS = 32
PER_GROUP = C // GROUPS
CAP = 3
HH = 32
WW = 8
PIX = HH * WW
ROWS = CAP * PIX
ENTRIES = PIX * PER_GROUP
VMEM = pltpu.VMEM
LANES = 128
HALF = 4 * C
PARAMS = pltpu.CompilerParams(vmem_limit_bytes=48 * 1024 * 1024)


def group_matrix():
    row = lax.broadcasted_iota(jnp.int32, (C, C), 0).astype(F32)
    col = lax.broadcasted_iota(jnp.int32, (C, C), 1).astype(F32)
    inv = 1.0 / PER_GROUP
    return (jnp.floor((row + 0.5) * inv) == jnp.floor((col + 0.5) * inv)).astype(F32)


def group_mean(sums, matrix):
    return (
        jnp.dot(sums, matrix, precision=lax.Precision.HIGHEST, preferred_element_type=F32) / ENTRIES
    )


def frame(s):
    return pl.ds(pl.multiple_of(s * PIX, PIX), PIX)


def sigmoid(values):
    return 0.5 * jnp.tanh(0.5 * values) + 0.5


def shifted(values, step):
    cube = values.reshape(HH, WW, C)
    rolled = jnp.roll(cube, -step, axis=1)
    col = lax.broadcasted_iota(jnp.int32, (HH, WW, C), 1)
    keep = (col < WW - 1) if step > 0 else (col > 0)
    return jnp.where(keep, rolled, 0.0).reshape(PIX, C)


def down(values):
    return jnp.concatenate([jnp.zeros((WW, C), F32), values[:-WW]], axis=0)


def up(values):
    return jnp.concatenate([values[WW:], jnp.zeros((WW, C), F32)], axis=0)


def forward_kernel(n_ref, x_ref, gain_ref, shift_ref, w_ref, y_ref, u_ref, stats_ref, cols, wst, prod):
    for i in range(3):
        wst[i * C : (i + 1) * C, :] = w_ref[:, i * 3 * C : (i + 1) * 3 * C]
    matrix = group_matrix()
    blank = jnp.zeros((8 - CAP, C), F32)

    def per_frame(fn):
        return jnp.concatenate([fn(s) for s in range(CAP)] + [blank], axis=0)

    def load(s):
        return x_ref[s * PIX : (s + 1) * PIX, :].astype(F32)

    mean = group_mean(per_frame(lambda s: jnp.sum(load(s), axis=0, keepdims=True)), matrix)

    def squares(s):
        centred = load(s) - mean[s : s + 1]
        return jnp.sum(centred * centred, axis=0, keepdims=True)

    inv = lax.rsqrt(group_mean(per_frame(squares), matrix) + 1e-05)
    stats_ref[0] = mean
    stats_ref[1] = inv

    def activate(s, carry):
        values = (x_ref[frame(s), :].astype(F32) - stats_ref[0, pl.ds(s, 1), :]) * stats_ref[
            1, pl.ds(s, 1), :
        ] * gain_ref[...] + shift_ref[...]
        act = values * sigmoid(values)
        cols[frame(s), 0:C] = shifted(act, -1).astype(BF16)
        cols[frame(s), C : 2 * C] = act.astype(BF16)
        cols[frame(s), 2 * C : 3 * C] = shifted(act, 1).astype(BF16)
        return carry

    lax.fori_loop(0, CAP, activate, 0)

    def convolve(s, carry):
        prod[...] = lax.dot_general(
            cols[frame(s), :], wst[...], (((1,), (1,)), ((), ())), preferred_element_type=F32
        )
        mixed = down(prod[:, 0:C]) + prod[:, C : 2 * C] + up(prod[:, 2 * C : 3 * C])
        y = (x_ref[frame(s), :].astype(F32) + mixed).astype(BF16)
        y_ref[frame(s), :] = y
        yf = y.astype(F32)
        live = (s < n_ref[0]).astype(F32)
        u_ref[frame(s), :] = (yf * sigmoid(yf) * live).astype(BF16)
        return carry

    lax.fori_loop(0, CAP, convolve, 0)


def extend(n, ext, g_ref, before_ref, after_ref):
    ext[0:PIX, :] = before_ref[...]
    ext[PIX : PIX + ROWS, :] = g_ref[...]
    ext[PIX + ROWS :, :] = after_ref[...]
    ext[frame(n + 1), :] = after_ref[...]


def grad_kernel(n_ref, core_ref, u_ref, g_ref, before_ref, after_ref, keep_ref, send_ref, ext, whole):
    extend(n_ref[0], ext, g_ref, before_ref, after_ref)
    flipped = ext[...].T
    whole[:, 2 * C + 2 * LANES :] = jnp.zeros((C, 8 * LANES - 2 * C - 2 * LANES), F32)
    for k in range(3):
        lo = (2 - k) * PIX
        whole[:, k * C : (k + 1) * C] = jnp.dot(
            flipped[:, lo : lo + ROWS], u_ref[...], preferred_element_type=F32
        )
    core = core_ref[0]
    for j in range(4):
        first = whole[:, j * LANES : (j + 1) * LANES]
        second = whole[:, (j + 4) * LANES : (j + 5) * LANES]
        keep_ref[j * C : (j + 1) * C, :] = jnp.where(core == 0, first, second)
        send_ref[j * C : (j + 1) * C, :] = jnp.where(core == 0, second, first).astype(BF16)


def backward_kernel(
    n_ref, x_ref, y_ref, g_ref, before_ref, after_ref, stats_ref, gain_ref, shift_ref, w_ref, wt_ref,
    out_ref, ext, cols, wst, prod, dys, grads,
):
    extend(n_ref[0], ext, g_ref, before_ref, after_ref)
    for i in range(3):
        for j in range(3):
            tap = 3 * i + j
            wst[j * C : (j + 1) * C, i * C : (i + 1) * C] = w_ref[:, tap * C : (tap + 1) * C]

    def temporal(s, carry):
        back = jnp.zeros((PIX, C), F32)
        for k in range(3):
            back = back + jnp.dot(
                ext[frame(s + 2 - k), :],
                wt_ref[:, k * C : (k + 1) * C],
                preferred_element_type=F32,
            )
        yf = y_ref[frame(s), :].astype(F32)
        sig = sigmoid(yf)
        back = (sig * (1.0 + yf * (1.0 - sig)) * back).astype(BF16)
        dy = (g_ref[frame(s), :].astype(F32) + back.astype(F32)).astype(BF16)
        dys[frame(s), :] = dy
        dyf = dy.astype(F32)
        cols[frame(s), 0:C] = shifted(dyf, 1).astype(BF16)
        cols[frame(s), C : 2 * C] = dy
        cols[frame(s), 2 * C : 3 * C] = shifted(dyf, -1).astype(BF16)
        return carry

    lax.fori_loop(0, CAP, temporal, 0)
    matrix = group_matrix()

    def finish(s, carry):
        prod[...] = jnp.dot(cols[frame(s), :], wst[...], preferred_element_type=F32)
        da = up(prod[:, 0:C]) + prod[:, C : 2 * C] + down(prod[:, 2 * C : 3 * C])
        mean = stats_ref[0, pl.ds(s, 1), :]
        inv = stats_ref[1, pl.ds(s, 1), :]
        normed = (x_ref[frame(s), :].astype(F32) - mean) * inv
        values = normed * gain_ref[...] + shift_ref[...]
        sig = sigmoid(values)
        dn = da * (sig * (1.0 + values * (1.0 - sig))) * gain_ref[...]
        sums = jnp.concatenate(
            [
                jnp.sum(dn, axis=0, keepdims=True),
                jnp.sum(dn * normed, axis=0, keepdims=True),
                jnp.zeros((6, C), F32),
            ],
            axis=0,
        )
        means = group_mean(sums, matrix)
        dx = inv * (dn - means[0:1] - normed * means[1:2])
        total = dys[frame(s), :].astype(F32) + dx
        out_ref[frame(s), :] = jnp.where(s < n_ref[0], total, 0.0).astype(BF16)
        return carry

    lax.fori_loop(0, CAP, finish, 0)


def final_kernel(scale, core_ref, mine_ref, other_ref, out_ref):
    core = core_ref[0]
    for j in range(4):
        mine = mine_ref[j * C : (j + 1) * C, :].astype(F32) * scale
        other = other_ref[j * C : (j + 1) * C, :].astype(F32) * scale
        out_ref[:, j * LANES : (j + 1) * LANES] = jnp.where(core == 0, mine, other)
        width = min(LANES, 3 * C - (j + 4) * LANES)
        upper = jnp.where(core == 0, other, mine)
        out_ref[:, (j + 4) * LANES : (j + 4) * LANES + width] = upper[:, :width]


SMEM_SPEC = pl.BlockSpec(memory_space=pltpu.SMEM)
VMEM_SPEC = pl.BlockSpec(memory_space=pltpu.VMEM)


def call(body, scalars, arrays, outs, scratch, cost):
    return pl.pallas_call(
        body,
        out_shape=outs,
        in_specs=[SMEM_SPEC] * len(scalars) + [VMEM_SPEC] * len(arrays),
        out_specs=[VMEM_SPEC] * len(outs) if isinstance(outs, list) else VMEM_SPEC,
        scratch_shapes=scratch,
        compiler_params=PARAMS,
        cost_estimate=pl.CostEstimate(flops=cost[0], bytes_accessed=cost[1], transcendentals=0),
    )(*scalars, *arrays)


def shards(frames_in, cotangent, counts, norm_gain, norm_shift, spatial_weight, temporal_weight):
    shape = frames_in.shape
    x = frames_in.reshape(ROWS, C)
    g = cotangent.reshape(ROWS, C)
    counts_row = counts[0]
    tm_size = lax.axis_size("tm")
    z_size = lax.axis_size("z")
    own = lax.dynamic_slice(counts_row, (lax.axis_index("tm"),), (1,))
    core = lax.axis_index("c").astype(jnp.int32).reshape(1)
    gain = norm_gain.reshape(1, C)
    shift = norm_shift.reshape(1, C)
    w_t = spatial_weight.T
    wt_t = temporal_weight.T

    last = lax.dynamic_slice(g, ((own[0] - 1) * PIX, 0), (PIX, C))
    before = lax.ppermute(last, "tm", [(t, t + 1) for t in range(tm_size - 1)])
    after = lax.ppermute(g[:PIX], "tm", [(t + 1, t) for t in range(tm_size - 1)])

    y, u, stats = call(
        forward_kernel,
        (own,),
        (x, gain, shift, w_t),
        [
            jax.ShapeDtypeStruct((ROWS, C), BF16),
            jax.ShapeDtypeStruct((ROWS, C), BF16),
            jax.ShapeDtypeStruct((2, 8, C), F32),
        ],
        [VMEM((ROWS, 3 * C), BF16), VMEM((3 * C, 3 * C), BF16), VMEM((PIX, 3 * C), F32)],
        (2 * ROWS * 9 * C * C, 4_000_000),
    )

    keep, send = call(
        grad_kernel,
        (own, core),
        (u, g, before, after),
        [jax.ShapeDtypeStruct((HALF, LANES), F32), jax.ShapeDtypeStruct((HALF, LANES), BF16)],
        [VMEM((5 * PIX, C), BF16), VMEM((C, 8 * LANES), F32)],
        (2 * ROWS * 3 * C * C, 2_500_000),
    )
    pair = [(0, 1), (1, 0)]
    got = lax.ppermute(send, "c", pair)
    part = (keep + got.astype(F32)).astype(BF16).reshape(tm_size, HALF // tm_size, LANES)
    part = lax.all_to_all(part, "tm", 0, 0, tiled=True)
    part = part.astype(F32).sum(axis=0).astype(BF16)
    part = lax.all_to_all(
        jnp.broadcast_to(part, (z_size,) + part.shape), "z", 0, 0, tiled=True
    )
    part = part.astype(F32).sum(axis=0).astype(BF16)
    part = lax.all_to_all(
        jnp.broadcast_to(part, (tm_size,) + part.shape), "tm", 0, 0, tiled=True
    )
    mine = part.reshape(HALF, LANES)
    other = lax.ppermute(mine, "c", pair)

    d_in = call(
        backward_kernel,
        (own,),
        (x, y, g, before, after, stats, gain, shift, w_t, wt_t),
        jax.ShapeDtypeStruct((ROWS, C), BF16),
        [
            VMEM((5 * PIX, C), BF16),
            VMEM((ROWS, 3 * C), BF16),
            VMEM((3 * C, 3 * C), BF16),
            VMEM((PIX, 3 * C), F32),
            VMEM((ROWS, C), BF16),
            VMEM((8, C), F32),
        ],
        (2 * ROWS * 12 * C * C, 5_000_000),
    )

    frames = lax.axis_size("z") * lax.axis_size("c") * 2 * tm_size
    scale = 1.0 / math.sqrt(frames * HH * WW)

    def finish(*refs):
        final_kernel(scale, *refs)

    grad = call(
        finish,
        (core,),
        (mine, other),
        jax.ShapeDtypeStruct((C, 3 * C), F32),
        [],
        (1_000_000, 2_000_000),
    )
    return (d_in.reshape(shape), grad.T)


def solution(mesh):
    devices = mesh.devices
    dp, tm = devices.shape
    split = Mesh(devices.reshape(dp // 2, 2, tm), ("z", "c", "tm"))
    return jax.shard_map(
        shards,
        mesh=split,
        in_specs=(
            P(("z", "c"), "tm", None, None, None),
            P(("z", "c"), "tm", None, None, None),
            P(("z", "c"), None),
            P(),
            P(),
            P(),
            P(),
        ),
        out_specs=(P(("z", "c"), "tm", None, None, None), P()),
        check_vma=False,
    )
```

```python
import math

import jax
import jax.numpy as jnp
from jax import lax
from jax.experimental import pallas as pl
from jax.experimental.pallas import tpu as pltpu
from jax.sharding import Mesh
from jax.sharding import PartitionSpec as P

F32 = jnp.float32
BF16 = jnp.bfloat16
C = 320
GROUPS = 32
PER_GROUP = C // GROUPS
CAP = 3
HH = 32
WW = 8
PIX = HH * WW
ROWS = CAP * PIX
ENTRIES = PIX * PER_GROUP
VMEM = pltpu.VMEM
LANES = 128
HALF = 4 * C
PARAMS = pltpu.CompilerParams(vmem_limit_bytes=28 * 1024 * 1024)


def group_matrix():
    row = lax.broadcasted_iota(jnp.int32, (C, C), 0).astype(F32)
    col = lax.broadcasted_iota(jnp.int32, (C, C), 1).astype(F32)
    inv = 1.0 / PER_GROUP
    same = jnp.floor((row + 0.5) * inv) == jnp.floor((col + 0.5) * inv)
    return same.astype(F32).astype(BF16)


def group_mean(sums, matrix):
    high = sums.astype(BF16).astype(F32)
    rest = sums - high
    middle = rest.astype(BF16).astype(F32)
    terms = jnp.concatenate([high, middle, rest - middle, jnp.zeros((8, C), F32)], axis=0)
    added = jnp.dot(terms.astype(BF16), matrix, preferred_element_type=F32)
    return (added[0:8] + added[8:16] + added[16:24]) / ENTRIES


def frame(s):
    return pl.ds(pl.multiple_of(s * PIX, PIX), PIX)


def sigmoid(values):
    return 0.5 * jnp.tanh(0.5 * values) + 0.5


def shifted(values, step):
    cube = values.reshape(HH, WW, C)
    rolled = jnp.roll(cube, -step, axis=1)
    col = lax.broadcasted_iota(jnp.int32, (HH, WW, C), 1)
    keep = (col < WW - 1) if step > 0 else (col > 0)
    return jnp.where(keep, rolled, 0.0).reshape(PIX, C)


def down(values):
    return jnp.concatenate([jnp.zeros((WW, C), F32), values[:-WW]], axis=0)


def up(values):
    return jnp.concatenate([values[WW:], jnp.zeros((WW, C), F32)], axis=0)


def start_all(sems, *pairs):
    copies = [pltpu.make_async_copy(src, dst, sems.at[i]) for i, (src, dst) in enumerate(pairs)]
    for copy in copies:
        copy.start()
    return copies


def edge_kernel(t_ref, counts_hbm, g_hbm, first_ref, last_ref, g_ref, counts, sems):
    for copy in start_all(sems, (counts_hbm, counts), (g_hbm, g_ref)):
        copy.wait()
    n = counts[0, t_ref[0]]
    first_ref[...] = g_ref[0:PIX, :]
    last_ref[...] = g_ref[frame(n - 1), :]


def forward_kernel(
    t_ref, counts_hbm, x_hbm, gain_hbm, shift_hbm, w_hbm, y_ref, u_ref, stats_ref,
    counts, x_ref, gain_ref, shift_ref, w_ref, cols, wst, prod, sems,
):
    copies = start_all(
        sems,
        (x_hbm, x_ref),
        (gain_hbm, gain_ref),
        (shift_hbm, shift_ref),
        (counts_hbm, counts),
        (w_hbm, w_ref),
    )
    matrix = group_matrix()
    blank = jnp.zeros((8 - CAP, C), F32)
    copies[0].wait()

    def per_frame(fn):
        return jnp.concatenate([fn(s) for s in range(CAP)] + [blank], axis=0)

    def load(s):
        return x_ref[s * PIX : (s + 1) * PIX, :].astype(F32)

    mean = group_mean(per_frame(lambda s: jnp.sum(load(s), axis=0, keepdims=True)), matrix)

    def squares(s):
        centred = load(s) - mean[s : s + 1]
        return jnp.sum(centred * centred, axis=0, keepdims=True)

    inv = lax.rsqrt(group_mean(per_frame(squares), matrix) + 1e-05)
    stats_ref[0] = mean
    stats_ref[1] = inv
    for copy in copies[1:4]:
        copy.wait()
    n = counts[0, t_ref[0]]
    gain = gain_ref[...].reshape(1, C)
    shift = shift_ref[...].reshape(1, C)

    def activate(s, carry):
        values = (x_ref[frame(s), :].astype(F32) - stats_ref[0, pl.ds(s, 1), :]) * stats_ref[
            1, pl.ds(s, 1), :
        ] * gain + shift
        act = values * sigmoid(values)
        cols[frame(s), 0:C] = shifted(act, -1).astype(BF16)
        cols[frame(s), C : 2 * C] = act.astype(BF16)
        cols[frame(s), 2 * C : 3 * C] = shifted(act, 1).astype(BF16)
        return carry

    lax.fori_loop(0, CAP, activate, 0)
    copies[4].wait()
    for i in range(3):
        wst[i * C : (i + 1) * C, :] = w_ref[:, i * 3 * C : (i + 1) * 3 * C]
    prod[...] = lax.dot_general(
        cols[...], wst[...], (((1,), (1,)), ((), ())), preferred_element_type=F32
    )

    def add(s, carry):
        rows = frame(s)
        mixed = down(prod[rows, 0:C]) + prod[rows, C : 2 * C] + up(prod[rows, 2 * C : 3 * C])
        y = (x_ref[rows, :].astype(F32) + mixed).astype(BF16)
        y_ref[rows, :] = y
        yf = y.astype(F32)
        live = (s < n).astype(F32)
        u_ref[rows, :] = (yf * sigmoid(yf) * live).astype(BF16)
        return carry

    lax.fori_loop(0, CAP, add, 0)


def grad_kernel(
    t_ref, core_ref, u_ref, g_ref, before_ref, after_ref, counts_hbm, keep_ref, send_ref, ext,
    counts, whole, sems,
):
    (copy,) = start_all(sems, (counts_hbm, counts))
    ext[0:PIX, :] = before_ref[...]
    ext[PIX : PIX + ROWS, :] = g_ref[...]
    ext[PIX + ROWS :, :] = after_ref[...]
    copy.wait()
    n = counts[0, t_ref[0]]
    ext[frame(n + 1), :] = after_ref[...]
    flipped = ext[...].T
    whole[:, 2 * C + 2 * LANES :] = jnp.zeros((C, 8 * LANES - 2 * C - 2 * LANES), F32)
    for k in range(3):
        lo = (2 - k) * PIX
        whole[:, k * C : (k + 1) * C] = jnp.dot(
            flipped[:, lo : lo + ROWS], u_ref[...], preferred_element_type=F32
        )
    core = core_ref[0]
    for j in range(4):
        first = whole[:, j * LANES : (j + 1) * LANES]
        second = whole[:, (j + 4) * LANES : (j + 5) * LANES]
        keep_ref[j * C : (j + 1) * C, :] = jnp.where(core == 0, first, second)
        send_ref[j * C : (j + 1) * C, :] = jnp.where(core == 0, second, first).astype(BF16)


def temporal_kernel(y_ref, ext, wt_hbm, dy_ref, wt_ref, sems):
    (copy,) = start_all(sems, (wt_hbm, wt_ref))
    copy.wait()

    def body(s, carry):
        back = jnp.zeros((PIX, C), F32)
        for k in range(3):
            back = back + jnp.dot(
                ext[frame(s + 2 - k), :],
                wt_ref[:, k * C : (k + 1) * C],
                preferred_element_type=F32,
            )
        yf = y_ref[frame(s), :].astype(F32)
        sig = sigmoid(yf)
        back = (sig * (1.0 + yf * (1.0 - sig)) * back).astype(BF16)
        own = ext[frame(s + 1), :].astype(F32)
        dy_ref[frame(s), :] = (own + back.astype(F32)).astype(BF16)
        return carry

    lax.fori_loop(0, CAP, body, 0)


def spatial_kernel(
    t_ref, dy_ref, stats_ref, counts_hbm, x_hbm, gain_hbm, shift_hbm, w_hbm, out_ref,
    counts, x_ref, gain_ref, shift_ref, w_ref, cols, wst, prod, sems,
):
    copies = start_all(
        sems,
        (w_hbm, w_ref),
        (x_hbm, x_ref),
        (gain_hbm, gain_ref),
        (shift_hbm, shift_ref),
        (counts_hbm, counts),
    )

    def spread(s, carry):
        dy = dy_ref[frame(s), :]
        dyf = dy.astype(F32)
        cols[frame(s), 0:C] = shifted(dyf, 1).astype(BF16)
        cols[frame(s), C : 2 * C] = dy
        cols[frame(s), 2 * C : 3 * C] = shifted(dyf, -1).astype(BF16)
        return carry

    lax.fori_loop(0, CAP, spread, 0)
    copies[0].wait()
    for i in range(3):
        for j in range(3):
            tap = 3 * i + j
            wst[j * C : (j + 1) * C, i * C : (i + 1) * C] = w_ref[:, tap * C : (tap + 1) * C]
    prod[...] = jnp.dot(cols[...], wst[...], preferred_element_type=F32)
    matrix = group_matrix()
    for copy in copies[1:]:
        copy.wait()
    n = counts[0, t_ref[0]]
    gain = gain_ref[...].reshape(1, C)
    shift = shift_ref[...].reshape(1, C)

    def finish(s, carry):
        rows = frame(s)
        da = up(prod[rows, 0:C]) + prod[rows, C : 2 * C] + down(prod[rows, 2 * C : 3 * C])
        mean = stats_ref[0, pl.ds(s, 1), :]
        inv = stats_ref[1, pl.ds(s, 1), :]
        normed = (x_ref[rows, :].astype(F32) - mean) * inv
        values = normed * gain + shift
        sig = sigmoid(values)
        dn = da * (sig * (1.0 + values * (1.0 - sig))) * gain
        sums = jnp.concatenate(
            [
                jnp.sum(dn, axis=0, keepdims=True),
                jnp.sum(dn * normed, axis=0, keepdims=True),
                jnp.zeros((6, C), F32),
            ],
            axis=0,
        )
        means = group_mean(sums, matrix)
        dx = inv * (dn - means[0:1] - normed * means[1:2])
        total = dy_ref[rows, :].astype(F32) + dx
        out_ref[rows, :] = jnp.where(s < n, total, 0.0).astype(BF16)
        return carry

    lax.fori_loop(0, CAP, finish, 0)


def sum_kernel(copies, x_ref, out_ref):
    total = x_ref[0].astype(F32)
    for i in range(1, x_ref.shape[0]):
        total = total + x_ref[i].astype(F32)
    total = total.astype(BF16)
    for i in range(copies):
        out_ref[i] = total


def final_kernel(scale, core_ref, mine_ref, other_ref, out_ref):
    core = core_ref[0]
    for j in range(4):
        mine = mine_ref[j * C : (j + 1) * C, :].astype(F32) * scale
        other = other_ref[j * C : (j + 1) * C, :].astype(F32) * scale
        out_ref[:, j * LANES : (j + 1) * LANES] = jnp.where(core == 0, mine, other)
        width = min(LANES, 3 * C - (j + 4) * LANES)
        upper = jnp.where(core == 0, other, mine)
        out_ref[:, (j + 4) * LANES : (j + 4) * LANES + width] = upper[:, :width]


SMEM_SPEC = pl.BlockSpec(memory_space=pltpu.SMEM)
VMEM_SPEC = pl.BlockSpec(memory_space=pltpu.VMEM)
HBM_SPEC = pl.BlockSpec(memory_space=pltpu.HBM)


def call(body, scalars, arrays, away, outs, scratch, cost):
    away = [pltpu.with_memory_space_constraint(a, pltpu.HBM) for a in away]
    return pl.pallas_call(
        body,
        out_shape=outs,
        in_specs=[SMEM_SPEC] * len(scalars) + [VMEM_SPEC] * len(arrays) + [HBM_SPEC] * len(away),
        out_specs=[VMEM_SPEC] * len(outs) if isinstance(outs, list) else VMEM_SPEC,
        scratch_shapes=scratch,
        compiler_params=PARAMS,
        cost_estimate=pl.CostEstimate(flops=cost[0], bytes_accessed=cost[1], transcendentals=0),
    )(*scalars, *arrays, *away)


def shards(frames_in, cotangent, counts, norm_gain, norm_shift, spatial_weight, temporal_weight):
    shape = frames_in.shape
    x = frames_in.reshape(ROWS, C)
    g = cotangent.reshape(ROWS, C)
    tm_size = lax.axis_size("tm")
    z_size = lax.axis_size("z")
    place = lax.axis_index("tm").astype(jnp.int32).reshape(1)
    core = lax.axis_index("c").astype(jnp.int32).reshape(1)
    w_t = spatial_weight.T
    wt_t = temporal_weight.T
    array = jax.ShapeDtypeStruct
    dma = pltpu.SemaphoreType.DMA

    act = array((ROWS, C), BF16)
    one = array((PIX, C), BF16)
    counts_mem = pltpu.SMEM(counts.shape, jnp.int32)
    vector = VMEM((C,), F32)
    rows_mem = VMEM((ROWS, C), BF16)
    weights = VMEM((C, 9 * C), BF16)
    columns = VMEM((ROWS, 3 * C), BF16)
    stacked = VMEM((3 * C, 3 * C), BF16)
    product = VMEM((ROWS, 3 * C), F32)

    first, last, g_own = call(
        edge_kernel,
        (place,),
        (),
        (counts, g),
        [one, one, act],
        [counts_mem, dma((2,))],
        (0, 600_000),
    )
    before = lax.ppermute(last, "tm", [(t, t + 1) for t in range(tm_size - 1)])
    after = lax.ppermute(first, "tm", [(t + 1, t) for t in range(tm_size - 1)])

    y, u, stats = call(
        forward_kernel,
        (place,),
        (),
        (counts, x, norm_gain, norm_shift, w_t),
        [act, act, array((2, 8, C), F32)],
        [counts_mem, rows_mem, vector, vector, weights, columns, stacked, product, dma((5,))],
        (2 * ROWS * 9 * C * C, 4_000_000),
    )

    keep, send, ext = call(
        grad_kernel,
        (place, core),
        (u, g_own, before, after),
        (counts,),
        [
            array((HALF, LANES), F32),
            array((HALF, LANES), BF16),
            array((5 * PIX, C), BF16),
        ],
        [counts_mem, VMEM((C, 8 * LANES), F32), dma((1,))],
        (2 * ROWS * 3 * C * C, 2_500_000),
    )
    pair = [(0, 1), (1, 0)]

    def total(parts, copies):
        def body(*refs):
            sum_kernel(copies, *refs)

        return call(
            body,
            (),
            (parts,),
            (),
            array((copies,) + parts.shape[1:], BF16),
            [],
            (parts.size, 2 * parts.size),
        )

    got = lax.ppermute(send, "c", pair)
    part = (keep + got.astype(F32)).astype(BF16).reshape(tm_size, HALF // tm_size, LANES)
    dy = call(
        temporal_kernel,
        (),
        (y, ext),
        (wt_t,),
        act,
        [VMEM((C, 3 * C), BF16), dma((1,))],
        (2 * ROWS * 3 * C * C, 2_500_000),
    )
    part = lax.all_to_all(part, "tm", 0, 0, tiled=True)
    part, dy = lax.optimization_barrier((part, dy))
    part = total(part, z_size)
    part = total(lax.all_to_all(part, "z", 0, 0, tiled=True), tm_size)
    mine = lax.all_to_all(part, "tm", 0, 0, tiled=True).reshape(HALF, LANES)

    d_in = call(
        spatial_kernel,
        (place,),
        (dy, stats),
        (counts, x, norm_gain, norm_shift, w_t),
        act,
        [counts_mem, rows_mem, vector, vector, weights, columns, stacked, product, dma((5,))],
        (2 * ROWS * 9 * C * C, 4_000_000),
    )
    mine, d_in = lax.optimization_barrier((mine, d_in))
    other = lax.ppermute(mine, "c", pair)

    frames = z_size * lax.axis_size("c") * 2 * tm_size
    scale = 1.0 / math.sqrt(frames * HH * WW)

    def finish(*refs):
        final_kernel(scale, *refs)

    grad = call(
        finish,
        (core,),
        (mine, other),
        (),
        array((C, 3 * C), F32),
        [],
        (1_000_000, 2_000_000),
    )
    return (d_in.reshape(shape), grad.T)


def solution(mesh):
    devices = mesh.devices
    dp, tm = devices.shape
    split = Mesh(devices.reshape(dp // 2, 2, tm), ("z", "c", "tm"))
    return jax.shard_map(
        shards,
        mesh=split,
        in_specs=(
            P(("z", "c"), "tm", None, None, None),
            P(("z", "c"), "tm", None, None, None),
            P(("z", "c"), None),
            P(),
            P(),
            P(),
            P(),
        ),
        out_specs=(P(("z", "c"), "tm", None, None, None), P()),
        check_vma=False,
    )
```

```python
import math

import jax
import jax.numpy as jnp
from jax import lax
from jax.experimental import pallas as pl
from jax.experimental.pallas import tpu as pltpu
from jax.sharding import Mesh
from jax.sharding import PartitionSpec as P

F32 = jnp.float32
BF16 = jnp.bfloat16
C = 320
GROUPS = 32
PER_GROUP = C // GROUPS
CAP = 3
HH = 32
WW = 8
PIX = HH * WW
ROWS = CAP * PIX
ENTRIES = PIX * PER_GROUP
VMEM = pltpu.VMEM
LANES = 128
X_SIZE = 4
HALF = 4 * C
PARAMS = pltpu.CompilerParams(vmem_limit_bytes=28 * 1024 * 1024)


def group_matrix():
    row = lax.broadcasted_iota(jnp.int32, (C, C), 0).astype(F32)
    col = lax.broadcasted_iota(jnp.int32, (C, C), 1).astype(F32)
    inv = 1.0 / PER_GROUP
    same = jnp.floor((row + 0.5) * inv) == jnp.floor((col + 0.5) * inv)
    return same.astype(F32).astype(BF16)


def group_mean(sums, matrix):
    high = sums.astype(BF16).astype(F32)
    rest = sums - high
    middle = rest.astype(BF16).astype(F32)
    terms = jnp.concatenate([high, middle, rest - middle, jnp.zeros((8, C), F32)], axis=0)
    added = jnp.dot(terms.astype(BF16), matrix, preferred_element_type=F32)
    return (added[0:8] + added[8:16] + added[16:24]) / ENTRIES


def frame(s):
    if isinstance(s, int):
        return pl.ds(s * PIX, PIX)
    return pl.ds(pl.multiple_of(s * PIX, PIX), PIX)


def sigmoid(values):
    return 0.5 * jnp.tanh(0.5 * values) + 0.5


def shifted(values, step):
    cube = values.reshape(HH, WW, C)
    rolled = jnp.roll(cube, -step, axis=1)
    col = lax.broadcasted_iota(jnp.int32, (HH, WW, C), 1)
    keep = (col < WW - 1) if step > 0 else (col > 0)
    return jnp.where(keep, rolled, 0.0).reshape(PIX, C)


def down(values):
    return jnp.concatenate([jnp.zeros((WW, C), F32), values[:-WW]], axis=0)


def up(values):
    return jnp.concatenate([values[WW:], jnp.zeros((WW, C), F32)], axis=0)


def start_all(sems, *pairs):
    copies = [pltpu.make_async_copy(src, dst, sems.at[i]) for i, (src, dst) in enumerate(pairs)]
    for copy in copies:
        copy.start()
    return copies


def edge_kernel(
    t_ref, core_ref, counts_hbm, g_hbm, x_hbm, one_ref, two_ref, g_ref, x_ref, counts, sems
):
    for copy in start_all(sems, (counts_hbm, counts), (g_hbm, g_ref), (x_hbm, x_ref)):
        copy.wait()
    last = (counts[0, t_ref[0]] - 1) * (1 - core_ref[0])
    one_ref[...] = g_ref[frame(last), :]
    last = (counts[0, t_ref[0]] - 1) * core_ref[0]
    two_ref[...] = g_ref[frame(last), :]


def forward_kernel(
    t_ref, x_ref, counts_hbm, gain_hbm, shift_hbm, wt_hbm, w_hbm, y_ref, u_ref, stats_ref, wt_ref,
    counts, gain_ref, shift_ref, w_ref, cols, wst, prod, sems,
):
    weights = [(w_hbm.at[pl.ds(q, 80), :], w_ref.at[pl.ds(q, 80), :]) for q in range(0, C, 80)]
    copies = start_all(
        sems,
        (gain_hbm, gain_ref),
        (shift_hbm, shift_ref),
        (counts_hbm, counts),
        (wt_hbm, wt_ref),
        *weights,
    )
    matrix = group_matrix()
    blank = jnp.zeros((8 - CAP, C), F32)

    def per_frame(fn):
        return jnp.concatenate([fn(s) for s in range(CAP)] + [blank], axis=0)

    def load(s):
        return x_ref[s * PIX : (s + 1) * PIX, :].astype(F32)

    mean = group_mean(per_frame(lambda s: jnp.sum(load(s), axis=0, keepdims=True)), matrix)

    def squares(s):
        centred = load(s) - mean[s : s + 1]
        return jnp.sum(centred * centred, axis=0, keepdims=True)

    inv = lax.rsqrt(group_mean(per_frame(squares), matrix) + 1e-05)
    stats_ref[0] = mean
    stats_ref[1] = inv
    for copy in copies[:3]:
        copy.wait()
    n = counts[0, t_ref[0]]
    gain = gain_ref[...].reshape(1, C)
    shift = shift_ref[...].reshape(1, C)

    def activate(s):
        values = (x_ref[frame(s), :].astype(F32) - stats_ref[0, pl.ds(s, 1), :]) * stats_ref[
            1, pl.ds(s, 1), :
        ] * gain + shift
        act = values * sigmoid(values)
        cols[frame(s), 0:C] = shifted(act, -1).astype(BF16)
        cols[frame(s), C : 2 * C] = act.astype(BF16)
        cols[frame(s), 2 * C : 3 * C] = shifted(act, 1).astype(BF16)

    for s in range(CAP):
        activate(s)
    for copy in copies[4:]:
        copy.wait()
    for i in range(3):
        wst[i * C : (i + 1) * C, :] = w_ref[:, i * 3 * C : (i + 1) * 3 * C]
    prod[...] = lax.dot_general(
        cols[...], wst[...], (((1,), (1,)), ((), ())), preferred_element_type=F32
    )

    def add(s):
        rows = frame(s)
        mixed = down(prod[rows, 0:C]) + prod[rows, C : 2 * C] + up(prod[rows, 2 * C : 3 * C])
        y = (x_ref[rows, :].astype(F32) + mixed).astype(BF16)
        y_ref[rows, :] = y
        yf = y.astype(F32)
        live = (jnp.int32(s) < n).astype(F32)
        u_ref[rows, :] = (yf * sigmoid(yf) * live).astype(BF16)

    for s in range(CAP):
        add(s)
    copies[3].wait()


def own_kernel(t_ref, u_ref, g_ref, counts_hbm, whole_ref, counts, sems):
    (copy,) = start_all(sems, (counts_hbm, counts))
    copy.wait()
    n = counts[0, t_ref[0]]
    live = [(jnp.int32(s) < n).astype(BF16) for s in range(CAP)]
    flipped = jnp.concatenate([g_ref[frame(s), :] * live[s] for s in range(CAP)], axis=0).T
    whole_ref[:, 3 * C - 3 * C % LANES :] = jnp.zeros((C, 8 * LANES - 3 * C + 3 * C % LANES), F32)

    def term(own, taken):
        return jnp.dot(own, taken, preferred_element_type=F32)

    whole_ref[:, 0:C] = term(flipped[:, PIX:], u_ref[0 : ROWS - PIX, :])
    whole_ref[:, C : 2 * C] = term(flipped, u_ref[...])
    whole_ref[:, 2 * C : 3 * C] = term(flipped[:, 0 : ROWS - PIX], u_ref[PIX:, :])


def sides(core, one_ref, two_ref):
    before = jnp.where(core == 0, one_ref[...], two_ref[...])
    after = jnp.where(core == 0, two_ref[...], one_ref[...])
    return before, after


def grad_kernel(
    t_ref, core_ref, whole_ref, u_ref, one_ref, two_ref, counts_hbm, keep_ref, send_ref, counts,
    whole, sems,
):
    (copy,) = start_all(sems, (counts_hbm, counts))
    core = core_ref[0]
    before, after = sides(core, one_ref, two_ref)
    copy.wait()
    n = counts[0, t_ref[0]]
    whole[...] = whole_ref[...]
    whole[:, 0:C] += jnp.dot(after.T, u_ref[frame(n - 1), :], preferred_element_type=F32)
    whole[:, 2 * C : 3 * C] += jnp.dot(before.T, u_ref[0:PIX, :], preferred_element_type=F32)
    for j in range(4):
        first = whole[:, j * LANES : (j + 1) * LANES]
        second = whole[:, (j + 4) * LANES : (j + 5) * LANES]
        keep_ref[j * C : (j + 1) * C, :] = jnp.where(core == 0, first, second)
        send_ref[j * C : (j + 1) * C, :] = jnp.where(core == 0, second, first).astype(BF16)


def temporal_kernel(
    t_ref, core_ref, y_ref, g_ref, one_ref, two_ref, wt_ref, counts_hbm, dy_ref, ext, counts, sems
):
    (copy,) = start_all(sems, (counts_hbm, counts))
    before, after = sides(core_ref[0], one_ref, two_ref)
    ext[0:PIX, :] = before
    ext[PIX : PIX + ROWS, :] = g_ref[...]
    ext[PIX + ROWS :, :] = after
    copy.wait()
    ext[frame(counts[0, t_ref[0]] + 1), :] = after
    for s in range(CAP):
        back = jnp.zeros((PIX, C), F32)
        for k in range(3):
            back = back + jnp.dot(
                ext[frame(s + 2 - k), :],
                wt_ref[:, k * C : (k + 1) * C],
                preferred_element_type=F32,
            )
        yf = y_ref[frame(s), :].astype(F32)
        sig = sigmoid(yf)
        back = (sig * (1.0 + yf * (1.0 - sig)) * back).astype(BF16)
        dy_ref[frame(s), :] = (g_ref[frame(s), :].astype(F32) + back.astype(F32)).astype(BF16)


def spatial_kernel(
    t_ref, dy_ref, stats_ref, x_ref, counts_hbm, gain_hbm, shift_hbm, w_hbm, out_ref,
    counts, gain_ref, shift_ref, w_ref, cols, wst, prod, sems,
):
    weights = [(w_hbm.at[pl.ds(q, 80), :], w_ref.at[pl.ds(q, 80), :]) for q in range(0, C, 80)]
    copies = start_all(
        sems,
        *weights,
        (gain_hbm, gain_ref),
        (shift_hbm, shift_ref),
        (counts_hbm, counts),
    )

    def spread(s):
        dy = dy_ref[frame(s), :]
        dyf = dy.astype(F32)
        cols[frame(s), 0:C] = shifted(dyf, 1).astype(BF16)
        cols[frame(s), C : 2 * C] = dy
        cols[frame(s), 2 * C : 3 * C] = shifted(dyf, -1).astype(BF16)

    for s in range(CAP):
        spread(s)
    for copy in copies:
        copy.wait()
    for i in range(3):
        for j in range(3):
            tap = 3 * i + j
            wst[j * C : (j + 1) * C, i * C : (i + 1) * C] = w_ref[:, tap * C : (tap + 1) * C]
    prod[...] = jnp.dot(cols[...], wst[...], preferred_element_type=F32)
    matrix = group_matrix()
    n = counts[0, t_ref[0]]
    gain = gain_ref[...].reshape(1, C)
    shift = shift_ref[...].reshape(1, C)

    def finish(s):
        rows = frame(s)
        da = up(prod[rows, 0:C]) + prod[rows, C : 2 * C] + down(prod[rows, 2 * C : 3 * C])
        mean = stats_ref[0, pl.ds(s, 1), :]
        inv = stats_ref[1, pl.ds(s, 1), :]
        normed = (x_ref[rows, :].astype(F32) - mean) * inv
        values = normed * gain + shift
        sig = sigmoid(values)
        dn = da * (sig * (1.0 + values * (1.0 - sig))) * gain
        sums = jnp.concatenate(
            [
                jnp.sum(dn, axis=0, keepdims=True),
                jnp.sum(dn * normed, axis=0, keepdims=True),
                jnp.zeros((6, C), F32),
            ],
            axis=0,
        )
        means = group_mean(sums, matrix)
        dx = inv * (dn - means[0:1] - normed * means[1:2])
        total = dy_ref[rows, :].astype(F32) + dx
        out_ref[rows, :] = jnp.where(jnp.int32(s) < n, total, 0.0).astype(BF16)

    for s in range(CAP):
        finish(s)


def sum_kernel(copies, x_ref, out_ref):
    total = x_ref[0].astype(F32)
    for i in range(1, x_ref.shape[0]):
        total = total + x_ref[i].astype(F32)
    total = total.astype(BF16)
    for i in range(copies):
        out_ref[i] = total


def final_kernel(scale, core_ref, mine_ref, other_ref, out_ref):
    core = core_ref[0]
    for j in range(4):
        mine = mine_ref[j * C : (j + 1) * C, :].astype(F32) * scale
        other = other_ref[j * C : (j + 1) * C, :].astype(F32) * scale
        out_ref[:, j * LANES : (j + 1) * LANES] = jnp.where(core == 0, mine, other)
        width = min(LANES, 3 * C - (j + 4) * LANES)
        upper = jnp.where(core == 0, other, mine)
        out_ref[:, (j + 4) * LANES : (j + 4) * LANES + width] = upper[:, :width]


SMEM_SPEC = pl.BlockSpec(memory_space=pltpu.SMEM)
VMEM_SPEC = pl.BlockSpec(memory_space=pltpu.VMEM)
HBM_SPEC = pl.BlockSpec(memory_space=pltpu.HBM)


def call(body, scalars, arrays, away, outs, scratch, cost):
    away = [pltpu.with_memory_space_constraint(a, pltpu.HBM) for a in away]
    return pl.pallas_call(
        body,
        out_shape=outs,
        in_specs=[SMEM_SPEC] * len(scalars) + [VMEM_SPEC] * len(arrays) + [HBM_SPEC] * len(away),
        out_specs=[VMEM_SPEC] * len(outs) if isinstance(outs, list) else VMEM_SPEC,
        scratch_shapes=scratch,
        compiler_params=PARAMS,
        cost_estimate=pl.CostEstimate(flops=cost[0], bytes_accessed=cost[1], transcendentals=0),
    )(*scalars, *arrays, *away)


array = jax.ShapeDtypeStruct
dma = pltpu.SemaphoreType.DMA
ACT = array((ROWS, C), BF16)
ONE = array((PIX, C), BF16)
VECTOR = VMEM((C,), F32)
WEIGHTS = VMEM((C, 9 * C), BF16)
COLUMNS = VMEM((ROWS, 3 * C), BF16)
STACKED = VMEM((3 * C, 3 * C), BF16)
PRODUCT = VMEM((ROWS, 3 * C), F32)


def counts_mem(counts):
    return pltpu.SMEM(counts.shape, jnp.int32)


def run_edge(place, core, counts, g, x):
    return call(
        edge_kernel,
        (place, core),
        (),
        (counts, g, x),
        [ONE, ONE, ACT, ACT],
        [counts_mem(counts), dma((3,))],
        (0, 1_200_000),
    )


def run_forward(place, counts, x, gain, shift, wt_t, w_t):
    return call(
        forward_kernel,
        (place,),
        (x,),
        (counts, gain, shift, wt_t, w_t),
        [ACT, ACT, array((2, 8, C), F32), array(wt_t.shape, BF16)],
        [counts_mem(counts), VECTOR, VECTOR, WEIGHTS, COLUMNS, STACKED, PRODUCT, dma((8,))],
        (2 * ROWS * 9 * C * C, 4_000_000),
    )


def run_own(place, u, g_own, counts):
    return call(
        own_kernel,
        (place,),
        (u, g_own),
        (counts,),
        array((C, 8 * LANES), F32),
        [counts_mem(counts), dma((1,))],
        (2 * ROWS * 3 * C * C, 2_500_000),
    )


def run_grad(place, core, whole, u, one, two, counts):
    return call(
        grad_kernel,
        (place, core),
        (whole, u, one, two),
        (counts,),
        [array((HALF, LANES), F32), array((HALF, LANES), BF16)],
        [counts_mem(counts), VMEM((C, 8 * LANES), F32), dma((1,))],
        (4 * PIX * C * C, 2_500_000),
    )


def run_temporal(place, core, y, g_own, one, two, wt_own, counts):
    return call(
        temporal_kernel,
        (place, core),
        (y, g_own, one, two, wt_own),
        (counts,),
        ACT,
        [VMEM((5 * PIX, C), BF16), counts_mem(counts), dma((1,))],
        (2 * ROWS * 3 * C * C, 2_500_000),
    )


def run_spatial(place, dy, stats, x, counts, gain, shift, w_t):
    return call(
        spatial_kernel,
        (place,),
        (dy, stats, x),
        (counts, gain, shift, w_t),
        ACT,
        [counts_mem(counts), VECTOR, VECTOR, WEIGHTS, COLUMNS, STACKED, PRODUCT, dma((7,))],
        (2 * ROWS * 9 * C * C, 4_000_000),
    )


def run_sum(parts, copies):
    def body(*refs):
        sum_kernel(copies, *refs)

    out = array((copies,) + parts.shape[1:], BF16)
    return call(body, (), (parts,), (), out, [], (parts.size, 2 * parts.size))


def run_final(scale, core, mine, other):
    def body(*refs):
        final_kernel(scale, *refs)

    return call(body, (core,), (mine, other), (), array((C, 3 * C), F32), [], (1_000_000, 2_000_000))


def shards(frames_in, cotangent, counts, norm_gain, norm_shift, spatial_weight, temporal_weight):
    shape = frames_in.shape
    x = frames_in.reshape(ROWS, C)
    g = cotangent.reshape(ROWS, C)
    place = lax.axis_index("tm").astype(jnp.int32).reshape(1)
    core = lax.axis_index("c").astype(jnp.int32).reshape(1)
    w_t = spatial_weight.T
    wt_t = temporal_weight.T
    tm_size = lax.axis_size("tm")
    pair = [(0, 1), (1, 0)]
    right = [[(c * tm_size + t, c * tm_size + t + 1) for t in range(tm_size - 1)] for c in range(2)]
    left = [[(b, a) for a, b in line] for line in right]

    one, two, g_own, x_own = run_edge(place, core, counts, g, x)
    one = lax.ppermute(one, ("c", "tm"), right[0] + left[1])
    two = lax.ppermute(two, ("c", "tm"), left[0] + right[1])
    y, u, stats, wt_own = run_forward(
        place, counts, x_own, norm_gain, norm_shift, wt_t, w_t
    )
    whole = run_own(place, u, g_own, counts)
    keep, send = run_grad(place, core, whole, u, one, two, counts)

    near, far = groups()
    size = len(near[0])
    got = lax.ppermute(send, "c", pair)
    part = (keep + got.astype(F32)).astype(BF16).reshape(size, HALF // size, LANES)
    part = run_sum(exchange(part, near), len(far[0]))
    part, one = lax.optimization_barrier((part, one))
    dy = run_temporal(place, core, y, g_own, one, two, wt_own, counts)
    d_in = run_spatial(place, dy, stats, x_own, counts, norm_gain, norm_shift, w_t)
    part, d_in = lax.optimization_barrier((exchange(part, far), d_in))
    part = run_sum(part, size)
    mine = exchange(part, near).reshape(HALF, LANES)
    other = lax.ppermute(mine, "c", pair)

    frames = lax.axis_size(("z", "c")) * 2 * tm_size
    grad = run_final(1.0 / math.sqrt(frames * HH * WW), core, mine, other)
    return (d_in.reshape(shape), grad.T)


def groups():
    zs, ys, xs = lax.axis_size("z"), lax.axis_size("tm") // X_SIZE, X_SIZE

    def at(z, c, y, x):
        return ((z * 2 + c) * ys + y) * xs + x

    near = [
        [at(z + i, c, y + j, x) for i in range(2) for j in range(2) for x in range(xs)]
        for z in range(0, zs, 2)
        for c in range(2)
        for y in range(0, ys, 2)
    ]
    far = [
        [at(z, c, y, x) for z in range(i, zs, 2) for y in range(j, ys, 2)]
        for i in range(2)
        for j in range(2)
        for c in range(2)
        for x in range(xs)
    ]
    return near, far


def exchange(parts, members):
    return lax.all_to_all(parts, ("z", "c", "tm"), 0, 0, axis_index_groups=members, tiled=True)


def solution(mesh):
    devices = mesh.devices
    dp, tm = devices.shape
    split = Mesh(devices.reshape(dp // 2, 2, tm), ("z", "c", "tm"))
    return jax.shard_map(
        shards,
        mesh=split,
        in_specs=(
            P(("z", "c"), "tm", None, None, None),
            P(("z", "c"), "tm", None, None, None),
            P(("z", "c"), None),
            P(),
            P(),
            P(),
            P(),
        ),
        out_specs=(P(("z", "c"), "tm", None, None, None), P()),
        check_vma=False,
    )
```

```python
import math

import jax
import jax.numpy as jnp
from jax import lax
from jax.experimental import pallas as pl
from jax.experimental.pallas import tpu as pltpu
from jax.sharding import Mesh
from jax.sharding import PartitionSpec as P

F32 = jnp.float32
BF16 = jnp.bfloat16
C = 320
GROUPS = 32
PER_GROUP = C // GROUPS
CAP = 3
HH = 32
WW = 8
PIX = HH * WW
ROWS = CAP * PIX
ENTRIES = PIX * PER_GROUP
VMEM = pltpu.VMEM
LANES = 128
X_SIZE = 4
HALF = 4 * C
PARAMS = pltpu.CompilerParams(vmem_limit_bytes=28 * 1024 * 1024)


def group_matrix():
    row = lax.broadcasted_iota(jnp.int32, (C, C), 0).astype(F32)
    col = lax.broadcasted_iota(jnp.int32, (C, C), 1).astype(F32)
    inv = 1.0 / PER_GROUP
    same = jnp.floor((row + 0.5) * inv) == jnp.floor((col + 0.5) * inv)
    return same.astype(F32).astype(BF16)


def group_mean(sums, matrix):
    high = sums.astype(BF16).astype(F32)
    rest = sums - high
    middle = rest.astype(BF16).astype(F32)
    terms = jnp.concatenate([high, middle, rest - middle, jnp.zeros((8, C), F32)], axis=0)
    added = jnp.dot(terms.astype(BF16), matrix, preferred_element_type=F32)
    return (added[0:8] + added[8:16] + added[16:24]) / ENTRIES


def frame(s):
    if isinstance(s, int):
        return pl.ds(s * PIX, PIX)
    return pl.ds(pl.multiple_of(s * PIX, PIX), PIX)


def sigmoid(values):
    return 0.5 * jnp.tanh(0.5 * values) + 0.5


def shifted(values, step):
    cube = values.reshape(HH, WW, C)
    rolled = jnp.roll(cube, -step, axis=1)
    col = lax.broadcasted_iota(jnp.int32, (HH, WW, C), 1)
    keep = (col < WW - 1) if step > 0 else (col > 0)
    return jnp.where(keep, rolled, 0.0).reshape(PIX, C)


def down(values):
    return jnp.concatenate([jnp.zeros((WW, C), F32), values[:-WW]], axis=0)


def up(values):
    return jnp.concatenate([values[WW:], jnp.zeros((WW, C), F32)], axis=0)


def start_all(sems, *pairs):
    copies = [pltpu.make_async_copy(src, dst, sems.at[i]) for i, (src, dst) in enumerate(pairs)]
    for copy in copies:
        copy.start()
    return copies


def packed(values):
    half = PIX // 2
    rest = values[:, 2 * LANES :]
    rest = jnp.concatenate([rest[:half], rest[half:]], axis=1)
    return jnp.concatenate([values[:, :LANES], values[:, LANES : 2 * LANES], rest], axis=0)


def unpacked(values):
    rest = values[2 * PIX :, :]
    tail = C - 2 * LANES
    rest = jnp.concatenate([rest[:, :tail], rest[:, tail:]], axis=0)
    return jnp.concatenate([values[:PIX], values[PIX : 2 * PIX], rest], axis=1)


def edge_kernel(
    t_ref, core_ref, counts_hbm, g_hbm, x_hbm, one_ref, two_ref, g_ref, x_ref, counts, sems
):
    for copy in start_all(sems, (counts_hbm, counts), (g_hbm, g_ref), (x_hbm, x_ref)):
        copy.wait()
    last = (counts[0, t_ref[0]] - 1) * (1 - core_ref[0])
    one_ref[...] = packed(g_ref[frame(last), :])
    last = (counts[0, t_ref[0]] - 1) * core_ref[0]
    two_ref[...] = packed(g_ref[frame(last), :])


def forward_kernel(
    t_ref, x_ref, counts_hbm, gain_hbm, shift_hbm, wt_hbm, w_hbm, y_ref, u_ref, stats_ref, wt_ref,
    counts, gain_ref, shift_ref, w_ref, cols, wst, prod, sems,
):
    weights = [(w_hbm.at[pl.ds(q, 80), :], w_ref.at[pl.ds(q, 80), :]) for q in range(0, C, 80)]
    copies = start_all(
        sems,
        (gain_hbm, gain_ref),
        (shift_hbm, shift_ref),
        (counts_hbm, counts),
        (wt_hbm, wt_ref),
        *weights,
    )
    matrix = group_matrix()
    blank = jnp.zeros((8 - CAP, C), F32)

    def per_frame(fn):
        return jnp.concatenate([fn(s) for s in range(CAP)] + [blank], axis=0)

    def load(s):
        return x_ref[s * PIX : (s + 1) * PIX, :].astype(F32)

    mean = group_mean(per_frame(lambda s: jnp.sum(load(s), axis=0, keepdims=True)), matrix)

    def squares(s):
        centred = load(s) - mean[s : s + 1]
        return jnp.sum(centred * centred, axis=0, keepdims=True)

    inv = lax.rsqrt(group_mean(per_frame(squares), matrix) + 1e-05)
    stats_ref[0] = mean
    stats_ref[1] = inv
    for copy in copies[:3]:
        copy.wait()
    n = counts[0, t_ref[0]]
    gain = gain_ref[...].reshape(1, C)
    shift = shift_ref[...].reshape(1, C)

    def activate(s):
        values = (x_ref[frame(s), :].astype(F32) - stats_ref[0, pl.ds(s, 1), :]) * stats_ref[
            1, pl.ds(s, 1), :
        ] * gain + shift
        act = values * sigmoid(values)
        cols[frame(s), 0:C] = shifted(act, -1).astype(BF16)
        cols[frame(s), C : 2 * C] = act.astype(BF16)
        cols[frame(s), 2 * C : 3 * C] = shifted(act, 1).astype(BF16)

    for s in range(CAP):
        activate(s)
    for copy in copies[4:]:
        copy.wait()
    for i in range(3):
        wst[i * C : (i + 1) * C, :] = w_ref[:, i * 3 * C : (i + 1) * 3 * C]
    prod[...] = lax.dot_general(
        cols[...], wst[...], (((1,), (1,)), ((), ())), preferred_element_type=F32
    )

    def add(s):
        rows = frame(s)
        mixed = down(prod[rows, 0:C]) + prod[rows, C : 2 * C] + up(prod[rows, 2 * C : 3 * C])
        y = (x_ref[rows, :].astype(F32) + mixed).astype(BF16)
        y_ref[rows, :] = y
        yf = y.astype(F32)
        live = (jnp.int32(s) < n).astype(F32)
        u_ref[rows, :] = (yf * sigmoid(yf) * live).astype(BF16)

    for s in range(CAP):
        add(s)
    copies[3].wait()


def own_kernel(t_ref, u_ref, g_ref, counts_hbm, whole_ref, counts, sems):
    (copy,) = start_all(sems, (counts_hbm, counts))
    copy.wait()
    n = counts[0, t_ref[0]]
    live = [(jnp.int32(s) < n).astype(BF16) for s in range(CAP)]
    flipped = jnp.concatenate([g_ref[frame(s), :] * live[s] for s in range(CAP)], axis=0).T
    whole_ref[:, 3 * C - 3 * C % LANES :] = jnp.zeros((C, 8 * LANES - 3 * C + 3 * C % LANES), F32)

    def term(own, taken):
        return jnp.dot(own, taken, preferred_element_type=F32)

    whole_ref[:, 0:C] = term(flipped[:, PIX:], u_ref[0 : ROWS - PIX, :])
    whole_ref[:, C : 2 * C] = term(flipped, u_ref[...])
    whole_ref[:, 2 * C : 3 * C] = term(flipped[:, 0 : ROWS - PIX], u_ref[PIX:, :])


def sides(core, one_ref, two_ref):
    before = jnp.where(core == 0, one_ref[...], two_ref[...])
    after = jnp.where(core == 0, two_ref[...], one_ref[...])
    return unpacked(before), unpacked(after)


def grad_kernel(
    t_ref, core_ref, whole_ref, u_ref, one_ref, two_ref, counts_hbm, keep_ref, send_ref, counts,
    whole, sems,
):
    (copy,) = start_all(sems, (counts_hbm, counts))
    core = core_ref[0]
    before, after = sides(core, one_ref, two_ref)
    copy.wait()
    n = counts[0, t_ref[0]]
    whole[...] = whole_ref[...]
    whole[:, 0:C] += jnp.dot(after.T, u_ref[frame(n - 1), :], preferred_element_type=F32)
    whole[:, 2 * C : 3 * C] += jnp.dot(before.T, u_ref[0:PIX, :], preferred_element_type=F32)
    for j in range(4):
        first = whole[:, j * LANES : (j + 1) * LANES]
        second = whole[:, (j + 4) * LANES : (j + 5) * LANES]
        keep_ref[j * C : (j + 1) * C, :] = jnp.where(core == 0, first, second)
        send_ref[j * C : (j + 1) * C, :] = jnp.where(core == 0, second, first).astype(BF16)


def temporal_kernel(
    t_ref, core_ref, y_ref, g_ref, one_ref, two_ref, wt_ref, counts_hbm, dy_ref, ext, counts, sems
):
    (copy,) = start_all(sems, (counts_hbm, counts))
    before, after = sides(core_ref[0], one_ref, two_ref)
    ext[0:PIX, :] = before
    ext[PIX : PIX + ROWS, :] = g_ref[...]
    ext[PIX + ROWS :, :] = after
    copy.wait()
    ext[frame(counts[0, t_ref[0]] + 1), :] = after
    for s in range(CAP):
        back = jnp.zeros((PIX, C), F32)
        for k in range(3):
            back = back + jnp.dot(
                ext[frame(s + 2 - k), :],
                wt_ref[:, k * C : (k + 1) * C],
                preferred_element_type=F32,
            )
        yf = y_ref[frame(s), :].astype(F32)
        sig = sigmoid(yf)
        back = (sig * (1.0 + yf * (1.0 - sig)) * back).astype(BF16)
        dy_ref[frame(s), :] = (g_ref[frame(s), :].astype(F32) + back.astype(F32)).astype(BF16)


def spatial_kernel(
    t_ref, dy_ref, stats_ref, x_ref, counts_hbm, gain_hbm, shift_hbm, w_hbm, out_ref,
    counts, gain_ref, shift_ref, w_ref, cols, wst, prod, sems,
):
    weights = [(w_hbm.at[pl.ds(q, 80), :], w_ref.at[pl.ds(q, 80), :]) for q in range(0, C, 80)]
    copies = start_all(
        sems,
        *weights,
        (gain_hbm, gain_ref),
        (shift_hbm, shift_ref),
        (counts_hbm, counts),
    )

    def spread(s):
        dy = dy_ref[frame(s), :]
        dyf = dy.astype(F32)
        cols[frame(s), 0:C] = shifted(dyf, 1).astype(BF16)
        cols[frame(s), C : 2 * C] = dy
        cols[frame(s), 2 * C : 3 * C] = shifted(dyf, -1).astype(BF16)

    for s in range(CAP):
        spread(s)
    for copy in copies:
        copy.wait()
    for i in range(3):
        for j in range(3):
            tap = 3 * i + j
            wst[j * C : (j + 1) * C, i * C : (i + 1) * C] = w_ref[:, tap * C : (tap + 1) * C]
    prod[...] = jnp.dot(cols[...], wst[...], preferred_element_type=F32)
    matrix = group_matrix()
    n = counts[0, t_ref[0]]
    gain = gain_ref[...].reshape(1, C)
    shift = shift_ref[...].reshape(1, C)

    def finish(s):
        rows = frame(s)
        da = up(prod[rows, 0:C]) + prod[rows, C : 2 * C] + down(prod[rows, 2 * C : 3 * C])
        mean = stats_ref[0, pl.ds(s, 1), :]
        inv = stats_ref[1, pl.ds(s, 1), :]
        normed = (x_ref[rows, :].astype(F32) - mean) * inv
        values = normed * gain + shift
        sig = sigmoid(values)
        dn = da * (sig * (1.0 + values * (1.0 - sig))) * gain
        sums = jnp.concatenate(
            [
                jnp.sum(dn, axis=0, keepdims=True),
                jnp.sum(dn * normed, axis=0, keepdims=True),
                jnp.zeros((6, C), F32),
            ],
            axis=0,
        )
        means = group_mean(sums, matrix)
        dx = inv * (dn - means[0:1] - normed * means[1:2])
        total = dy_ref[rows, :].astype(F32) + dx
        out_ref[rows, :] = jnp.where(jnp.int32(s) < n, total, 0.0).astype(BF16)

    for s in range(CAP):
        finish(s)


def add_kernel(core_ref, keep_ref, both_ref, out_ref):
    got = jnp.where(core_ref[0] == 0, both_ref[1], both_ref[0])
    out_ref[...] = (keep_ref[...] + got.astype(F32)).astype(BF16)


def sum_kernel(copies, x_ref, out_ref):
    total = x_ref[0].astype(F32)
    for i in range(1, x_ref.shape[0]):
        total = total + x_ref[i].astype(F32)
    total = total.astype(BF16)
    for i in range(copies):
        out_ref[i] = total


def final_kernel(scale, both_ref, out_ref):
    for j in range(8):
        width = min(LANES, 3 * C - j * LANES)
        rows = (j % 4) * C
        part = both_ref[j // 4, rows : rows + C, :].astype(F32) * scale
        out_ref[:, j * LANES : j * LANES + width] = part[:, :width]


SMEM_SPEC = pl.BlockSpec(memory_space=pltpu.SMEM)
VMEM_SPEC = pl.BlockSpec(memory_space=pltpu.VMEM)
HBM_SPEC = pl.BlockSpec(memory_space=pltpu.HBM)


def call(body, scalars, arrays, away, outs, scratch, cost):
    away = [pltpu.with_memory_space_constraint(a, pltpu.HBM) for a in away]
    return pl.pallas_call(
        body,
        out_shape=outs,
        in_specs=[SMEM_SPEC] * len(scalars) + [VMEM_SPEC] * len(arrays) + [HBM_SPEC] * len(away),
        out_specs=[VMEM_SPEC] * len(outs) if isinstance(outs, list) else VMEM_SPEC,
        scratch_shapes=scratch,
        compiler_params=PARAMS,
        cost_estimate=pl.CostEstimate(flops=cost[0], bytes_accessed=cost[1], transcendentals=0),
    )(*scalars, *arrays, *away)


array = jax.ShapeDtypeStruct
dma = pltpu.SemaphoreType.DMA
ACT = array((ROWS, C), BF16)
ONE = array((PIX * C // LANES, LANES), BF16)
VECTOR = VMEM((C,), F32)
WEIGHTS = VMEM((C, 9 * C), BF16)
COLUMNS = VMEM((ROWS, 3 * C), BF16)
STACKED = VMEM((3 * C, 3 * C), BF16)
PRODUCT = VMEM((ROWS, 3 * C), F32)


def counts_mem(counts):
    return pltpu.SMEM(counts.shape, jnp.int32)


def run_edge(place, core, counts, g, x):
    return call(
        edge_kernel,
        (place, core),
        (),
        (counts, g, x),
        [ONE, ONE, ACT, ACT],
        [counts_mem(counts), dma((3,))],
        (0, 1_200_000),
    )


def run_forward(place, counts, x, gain, shift, wt_t, w_t):
    return call(
        forward_kernel,
        (place,),
        (x,),
        (counts, gain, shift, wt_t, w_t),
        [ACT, ACT, array((2, 8, C), F32), array(wt_t.shape, BF16)],
        [counts_mem(counts), VECTOR, VECTOR, WEIGHTS, COLUMNS, STACKED, PRODUCT, dma((8,))],
        (2 * ROWS * 9 * C * C, 4_000_000),
    )


def run_own(place, u, g_own, counts):
    return call(
        own_kernel,
        (place,),
        (u, g_own),
        (counts,),
        array((C, 8 * LANES), F32),
        [counts_mem(counts), dma((1,))],
        (2 * ROWS * 3 * C * C, 2_500_000),
    )


def run_grad(place, core, whole, u, one, two, counts):
    return call(
        grad_kernel,
        (place, core),
        (whole, u, one, two),
        (counts,),
        [array((HALF, LANES), F32), array((HALF, LANES), BF16)],
        [counts_mem(counts), VMEM((C, 8 * LANES), F32), dma((1,))],
        (4 * PIX * C * C, 2_500_000),
    )


def run_temporal(place, core, y, g_own, one, two, wt_own, counts):
    return call(
        temporal_kernel,
        (place, core),
        (y, g_own, one, two, wt_own),
        (counts,),
        ACT,
        [VMEM((5 * PIX, C), BF16), counts_mem(counts), dma((1,))],
        (2 * ROWS * 3 * C * C, 2_500_000),
    )


def run_spatial(place, dy, stats, x, counts, gain, shift, w_t):
    return call(
        spatial_kernel,
        (place,),
        (dy, stats, x),
        (counts, gain, shift, w_t),
        ACT,
        [counts_mem(counts), VECTOR, VECTOR, WEIGHTS, COLUMNS, STACKED, PRODUCT, dma((7,))],
        (2 * ROWS * 9 * C * C, 4_000_000),
    )


def run_sum(parts, copies):
    def body(*refs):
        sum_kernel(copies, *refs)

    out = array((copies,) + parts.shape[1:], BF16)
    return call(body, (), (parts,), (), out, [], (parts.size, 2 * parts.size))


def run_add(core, keep, both):
    out = array(keep.shape, BF16)
    return call(add_kernel, (core,), (keep, both), (), out, [], (keep.size, 8 * keep.size))


def run_final(scale, both):
    def body(*refs):
        final_kernel(scale, *refs)

    return call(body, (), (both,), (), array((C, 3 * C), F32), [], (1_000_000, 2_000_000))


def shards(frames_in, cotangent, counts, norm_gain, norm_shift, spatial_weight, temporal_weight):
    shape = frames_in.shape
    x = frames_in.reshape(ROWS, C)
    g = cotangent.reshape(ROWS, C)
    place = lax.axis_index("tm").astype(jnp.int32).reshape(1)
    core = lax.axis_index("c").astype(jnp.int32).reshape(1)
    w_t = spatial_weight.T
    wt_t = temporal_weight.T
    tm_size = lax.axis_size("tm")
    right = [[(c * tm_size + t, c * tm_size + t + 1) for t in range(tm_size - 1)] for c in range(2)]
    left = [[(b, a) for a, b in line] for line in right]

    one, two, g_own, x_own = run_edge(place, core, counts, g, x)
    one = lax.ppermute(one, ("c", "tm"), right[0] + left[1])
    two = lax.ppermute(two, ("c", "tm"), left[0] + right[1])
    y, u, stats, wt_own = run_forward(
        place, counts, x_own, norm_gain, norm_shift, wt_t, w_t
    )
    whole = run_own(place, u, g_own, counts)
    keep, send = run_grad(place, core, whole, u, one, two, counts)

    near, far = groups()
    size = len(near[0])
    part = run_add(core, keep, lax.all_gather(send, "c")).reshape(size, HALF // size, LANES)
    part = run_sum(exchange(part, near), len(far[0]))
    part, one = lax.optimization_barrier((part, one))
    dy = run_temporal(place, core, y, g_own, one, two, wt_own, counts)
    d_in = run_spatial(place, dy, stats, x_own, counts, norm_gain, norm_shift, w_t)
    part, d_in = lax.optimization_barrier((exchange(part, far), d_in))
    part = run_sum(part, size)
    mine = exchange(part, near).reshape(HALF, LANES)
    both = lax.all_gather(mine, "c")

    frames = lax.axis_size(("z", "c")) * 2 * tm_size
    grad = run_final(1.0 / math.sqrt(frames * HH * WW), both)
    return (d_in.reshape(shape), grad.T)


def groups():
    zs, ys, xs = lax.axis_size("z"), lax.axis_size("tm") // X_SIZE, X_SIZE

    def at(z, c, y, x):
        return ((z * 2 + c) * ys + y) * xs + x

    near = [
        [at(z + i, c, y + j, x) for i in range(2) for j in range(2) for x in range(xs)]
        for z in range(0, zs, 2)
        for c in range(2)
        for y in range(0, ys, 2)
    ]
    far = [
        [at(z, c, y, x) for z in range(i, zs, 2) for y in range(j, ys, 2)]
        for i in range(2)
        for j in range(2)
        for c in range(2)
        for x in range(xs)
    ]
    return near, far


def exchange(parts, members):
    return lax.all_to_all(parts, ("z", "c", "tm"), 0, 0, axis_index_groups=members, tiled=True)


def solution(mesh):
    devices = mesh.devices
    dp, tm = devices.shape
    split = Mesh(devices.reshape(dp // 2, 2, tm), ("z", "c", "tm"))
    return jax.shard_map(
        shards,
        mesh=split,
        in_specs=(
            P(("z", "c"), "tm", None, None, None),
            P(("z", "c"), "tm", None, None, None),
            P(("z", "c"), None),
            P(),
            P(),
            P(),
            P(),
        ),
        out_specs=(P(("z", "c"), "tm", None, None, None), P()),
        check_vma=False,
    )
```

```python
import math

import jax
import jax.numpy as jnp
from jax import lax
from jax.experimental import pallas as pl
from jax.experimental.pallas import tpu as pltpu
from jax.sharding import Mesh
from jax.sharding import PartitionSpec as P

F32 = jnp.float32
BF16 = jnp.bfloat16
C = 320
GROUPS = 32
PER_GROUP = C // GROUPS
CAP = 3
HH = 32
WW = 8
PIX = HH * WW
ROWS = CAP * PIX
ENTRIES = PIX * PER_GROUP
VMEM = pltpu.VMEM
LANES = 128
X_SIZE = 4
HALF = 4 * C
PARAMS = pltpu.CompilerParams(vmem_limit_bytes=28 * 1024 * 1024)


def group_matrix():
    row = lax.broadcasted_iota(jnp.int32, (C, C), 0).astype(F32)
    col = lax.broadcasted_iota(jnp.int32, (C, C), 1).astype(F32)
    inv = 1.0 / PER_GROUP
    same = jnp.floor((row + 0.5) * inv) == jnp.floor((col + 0.5) * inv)
    return same.astype(F32).astype(BF16)


def group_mean(sums, matrix):
    high = sums.astype(BF16).astype(F32)
    rest = sums - high
    middle = rest.astype(BF16).astype(F32)
    terms = jnp.concatenate([high, middle, rest - middle, jnp.zeros((8, C), F32)], axis=0)
    added = jnp.dot(terms.astype(BF16), matrix, preferred_element_type=F32)
    return (added[0:8] + added[8:16] + added[16:24]) / ENTRIES


def frame(s):
    if isinstance(s, int):
        return pl.ds(s * PIX, PIX)
    return pl.ds(pl.multiple_of(s * PIX, PIX), PIX)


def sigmoid(values):
    return 0.5 * jnp.tanh(0.5 * values) + 0.5


def shifted(values, step):
    cube = values.reshape(HH, WW, C)
    rolled = jnp.roll(cube, -step, axis=1)
    col = lax.broadcasted_iota(jnp.int32, (HH, WW, C), 1)
    keep = (col < WW - 1) if step > 0 else (col > 0)
    return jnp.where(keep, rolled, 0.0).reshape(PIX, C)


def down(values):
    return jnp.concatenate([jnp.zeros((WW, C), F32), values[:-WW]], axis=0)


def up(values):
    return jnp.concatenate([values[WW:], jnp.zeros((WW, C), F32)], axis=0)


def start_all(sems, *pairs):
    copies = [pltpu.make_async_copy(src, dst, sems.at[i]) for i, (src, dst) in enumerate(pairs)]
    for copy in copies:
        copy.start()
    return copies


def packed(values):
    half = PIX // 2
    rest = values[:, 2 * LANES :]
    rest = jnp.concatenate([rest[:half], rest[half:]], axis=1)
    return jnp.concatenate([values[:, :LANES], values[:, LANES : 2 * LANES], rest], axis=0)


def unpacked(values):
    rest = values[2 * PIX :, :]
    tail = C - 2 * LANES
    rest = jnp.concatenate([rest[:, :tail], rest[:, tail:]], axis=0)
    return jnp.concatenate([values[:PIX], values[PIX : 2 * PIX], rest], axis=1)


def left_first(t_ref, core_ref):
    return lax.rem(t_ref[0] + core_ref[0], 2)


def edge_kernel(
    t_ref, core_ref, counts_hbm, g_hbm, one_ref, two_ref, g_ref, counts, sems
):
    frames = [(g_hbm.at[frame(s), :], g_ref.at[frame(s), :]) for s in range(CAP)]
    for copy in start_all(sems, (counts_hbm, counts), *frames):
        copy.wait()
    last = counts[0, t_ref[0]] - 1
    turn = left_first(t_ref, core_ref)
    one_ref[...] = packed(g_ref[frame(last * (1 - turn)), :])
    two_ref[...] = packed(g_ref[frame(last * turn), :])


def forward_kernel(
    t_ref, counts_hbm, x_hbm, gain_hbm, shift_hbm, wt_hbm, w_hbm, y_ref, u_ref, inner_ref, last_ref,
    stats_ref, wt_ref, x_ref, counts, gain_ref, shift_ref, w_ref, cols, wst, prod, sems,
):
    weights = [(w_hbm.at[pl.ds(q, 80), :], w_ref.at[pl.ds(q, 80), :]) for q in range(0, C, 80)]
    frames = [(x_hbm.at[frame(s), :], x_ref.at[frame(s), :]) for s in range(CAP)]
    copies = start_all(
        sems,
        *frames,
        (gain_hbm, gain_ref),
        (shift_hbm, shift_ref),
        (counts_hbm, counts),
        *weights,
        (wt_hbm, wt_ref),
    )
    matrix = group_matrix()
    blank = jnp.zeros((8 - CAP, C), F32)

    def per_frame(fn):
        return jnp.concatenate([fn(s) for s in range(CAP)] + [blank], axis=0)

    for copy in copies[:CAP]:
        copy.wait()

    def load(s):
        return x_ref[s * PIX : (s + 1) * PIX, :].astype(F32)

    mean = group_mean(per_frame(lambda s: jnp.sum(load(s), axis=0, keepdims=True)), matrix)

    def squares(s):
        centred = load(s) - mean[s : s + 1]
        return jnp.sum(centred * centred, axis=0, keepdims=True)

    inv = lax.rsqrt(group_mean(per_frame(squares), matrix) + 1e-05)
    stats_ref[0] = mean
    stats_ref[1] = inv
    for copy in copies[CAP : CAP + 3]:
        copy.wait()
    n = counts[0, t_ref[0]]
    gain = gain_ref[...].reshape(1, C)
    shift = shift_ref[...].reshape(1, C)

    def activate(s):
        values = (x_ref[frame(s), :].astype(F32) - stats_ref[0, pl.ds(s, 1), :]) * stats_ref[
            1, pl.ds(s, 1), :
        ] * gain + shift
        act = values * sigmoid(values)
        cols[frame(s), 0:C] = shifted(act, -1).astype(BF16)
        cols[frame(s), C : 2 * C] = act.astype(BF16)
        cols[frame(s), 2 * C : 3 * C] = shifted(act, 1).astype(BF16)

    for s in range(CAP):
        activate(s)
    for copy in copies[CAP + 3 : -1]:
        copy.wait()
    for i in range(3):
        wst[i * C : (i + 1) * C, :] = w_ref[:, i * 3 * C : (i + 1) * 3 * C]
    prod[...] = lax.dot_general(
        cols[...], wst[...], (((1,), (1,)), ((), ())), preferred_element_type=F32
    )

    zero = jnp.zeros((PIX, C), BF16)

    def add(s):
        rows = frame(s)
        mixed = down(prod[rows, 0:C]) + prod[rows, C : 2 * C] + up(prod[rows, 2 * C : 3 * C])
        y = (x_ref[rows, :].astype(F32) + mixed).astype(BF16)
        y_ref[rows, :] = y
        yf = y.astype(F32)
        units = (yf * sigmoid(yf)).astype(BF16)
        u_ref[rows, :] = jnp.where(jnp.int32(s) < n, units, zero)
        if s < CAP - 1:
            inner_ref[rows, :] = jnp.where(jnp.int32(s + 1) < n, units, zero)

    for s in range(CAP):
        add(s)
    last_ref[...] = u_ref[frame(n - 1), :]
    copies[-1].wait()


def own_kernel(u_ref, inner_ref, g_ref, whole_ref):
    flipped = g_ref[...].T
    whole_ref[:, 3 * C - 3 * C % LANES :] = jnp.zeros((C, 8 * LANES - 3 * C + 3 * C % LANES), F32)

    def term(own, taken):
        return jnp.dot(own, taken, preferred_element_type=F32)

    whole_ref[:, 0:C] = term(flipped[:, PIX:], inner_ref[...])
    whole_ref[:, C : 2 * C] = term(flipped, u_ref[...])
    whole_ref[:, 2 * C : 3 * C] = term(flipped[:, 0 : ROWS - PIX], u_ref[PIX:, :])


def sides(turn, one_ref, two_ref):
    before = jnp.where(turn == 1, one_ref[...], two_ref[...])
    after = jnp.where(turn == 1, two_ref[...], one_ref[...])
    return unpacked(before), unpacked(after)


def grad_kernel(
    t_ref, core_ref, whole_ref, u_ref, last_ref, one_ref, two_ref, keep_ref, send_ref, whole
):
    core = core_ref[0]
    before, after = sides(left_first(t_ref, core_ref), one_ref, two_ref)
    whole[...] = whole_ref[...]
    whole[:, 0:C] += jnp.dot(after.T, last_ref[...], preferred_element_type=F32)
    whole[:, 2 * C : 3 * C] += jnp.dot(before.T, u_ref[0:PIX, :], preferred_element_type=F32)
    for j in range(4):
        first = whole[:, j * LANES : (j + 1) * LANES]
        second = whole[:, (j + 4) * LANES : (j + 5) * LANES]
        keep_ref[j * C : (j + 1) * C, :] = jnp.where(core == 0, first, second)
        send_ref[j * C : (j + 1) * C, :] = jnp.where(core == 0, second, first).astype(BF16)


def temporal_kernel(
    t_ref, core_ref, y_ref, g_ref, one_ref, two_ref, wt_ref, counts_hbm, dy_ref, ext, counts, sems
):
    (copy,) = start_all(sems, (counts_hbm, counts))
    before, after = sides(left_first(t_ref, core_ref), one_ref, two_ref)
    ext[0:PIX, :] = before
    ext[PIX : PIX + ROWS, :] = g_ref[...]
    ext[PIX + ROWS :, :] = after
    copy.wait()
    ext[frame(counts[0, t_ref[0]] + 1), :] = after
    for s in range(CAP):
        back = jnp.zeros((PIX, C), F32)
        for k in range(3):
            back = back + jnp.dot(
                ext[frame(s + 2 - k), :],
                wt_ref[:, k * C : (k + 1) * C],
                preferred_element_type=F32,
            )
        yf = y_ref[frame(s), :].astype(F32)
        sig = sigmoid(yf)
        back = (sig * (1.0 + yf * (1.0 - sig)) * back).astype(BF16)
        dy_ref[frame(s), :] = (g_ref[frame(s), :].astype(F32) + back.astype(F32)).astype(BF16)


def spatial_kernel(
    t_ref, dy_ref, stats_ref, x_ref, counts_hbm, gain_hbm, shift_hbm, w_hbm, out_ref,
    counts, gain_ref, shift_ref, w_ref, cols, wst, prod, sems,
):
    weights = [(w_hbm.at[pl.ds(q, 80), :], w_ref.at[pl.ds(q, 80), :]) for q in range(0, C, 80)]
    copies = start_all(
        sems,
        *weights,
        (gain_hbm, gain_ref),
        (shift_hbm, shift_ref),
        (counts_hbm, counts),
    )

    def spread(s):
        dy = dy_ref[frame(s), :]
        dyf = dy.astype(F32)
        cols[frame(s), 0:C] = shifted(dyf, 1).astype(BF16)
        cols[frame(s), C : 2 * C] = dy
        cols[frame(s), 2 * C : 3 * C] = shifted(dyf, -1).astype(BF16)

    for s in range(CAP):
        spread(s)
    for copy in copies:
        copy.wait()
    for i in range(3):
        for j in range(3):
            tap = 3 * i + j
            wst[j * C : (j + 1) * C, i * C : (i + 1) * C] = w_ref[:, tap * C : (tap + 1) * C]
    prod[...] = jnp.dot(cols[...], wst[...], preferred_element_type=F32)
    matrix = group_matrix()
    n = counts[0, t_ref[0]]
    gain = gain_ref[...].reshape(1, C)
    shift = shift_ref[...].reshape(1, C)

    def finish(s):
        rows = frame(s)
        da = up(prod[rows, 0:C]) + prod[rows, C : 2 * C] + down(prod[rows, 2 * C : 3 * C])
        mean = stats_ref[0, pl.ds(s, 1), :]
        inv = stats_ref[1, pl.ds(s, 1), :]
        normed = (x_ref[rows, :].astype(F32) - mean) * inv
        values = normed * gain + shift
        sig = sigmoid(values)
        dn = da * (sig * (1.0 + values * (1.0 - sig))) * gain
        sums = jnp.concatenate(
            [
                jnp.sum(dn, axis=0, keepdims=True),
                jnp.sum(dn * normed, axis=0, keepdims=True),
                jnp.zeros((6, C), F32),
            ],
            axis=0,
        )
        means = group_mean(sums, matrix)
        dx = inv * (dn - means[0:1] - normed * means[1:2])
        total = dy_ref[rows, :].astype(F32) + dx
        out_ref[rows, :] = jnp.where(jnp.int32(s) < n, total, 0.0).astype(BF16)

    for s in range(CAP):
        finish(s)


def add_kernel(core_ref, keep_ref, both_ref, out_ref):
    got = jnp.where(core_ref[0] == 0, both_ref[1], both_ref[0])
    out_ref[...] = (keep_ref[...] + got.astype(F32)).astype(BF16)


def sum_kernel(copies, x_ref, out_ref):
    total = x_ref[0].astype(F32)
    for i in range(1, x_ref.shape[0]):
        total = total + x_ref[i].astype(F32)
    total = total.astype(BF16)
    for i in range(copies):
        out_ref[i] = total


def final_kernel(scale, both_ref, out_hbm, whole, sems):
    copies = []
    for i, row in enumerate(range(0, C, C // 4)):
        rows = pl.ds(row, C // 4)
        for j in range(8):
            width = min(LANES, 3 * C - j * LANES)
            start = (j % 4) * C + row
            part = both_ref[j // 4, start : start + C // 4, :].astype(F32) * scale
            whole[rows, j * LANES : j * LANES + width] = part[:, :width]
        copies.append(pltpu.make_async_copy(whole.at[rows, :], out_hbm.at[rows, :], sems.at[i]))
        copies[-1].start()
    for copy in copies:
        copy.wait()


SMEM_SPEC = pl.BlockSpec(memory_space=pltpu.SMEM)
VMEM_SPEC = pl.BlockSpec(memory_space=pltpu.VMEM)
HBM_SPEC = pl.BlockSpec(memory_space=pltpu.HBM)


def call(body, scalars, arrays, away, outs, scratch, cost, out_away=False):
    away = [pltpu.with_memory_space_constraint(a, pltpu.HBM) for a in away]
    out_spec = HBM_SPEC if out_away else VMEM_SPEC
    return pl.pallas_call(
        body,
        out_shape=outs,
        in_specs=[SMEM_SPEC] * len(scalars) + [VMEM_SPEC] * len(arrays) + [HBM_SPEC] * len(away),
        out_specs=[VMEM_SPEC] * len(outs) if isinstance(outs, list) else out_spec,
        scratch_shapes=scratch,
        compiler_params=PARAMS,
        cost_estimate=pl.CostEstimate(flops=cost[0], bytes_accessed=cost[1], transcendentals=0),
    )(*scalars, *arrays, *away)


array = jax.ShapeDtypeStruct
dma = pltpu.SemaphoreType.DMA
ACT = array((ROWS, C), BF16)
ONE = array((PIX * C // LANES, LANES), BF16)
VECTOR = VMEM((C,), F32)
WEIGHTS = VMEM((C, 9 * C), BF16)
COLUMNS = VMEM((ROWS, 3 * C), BF16)
STACKED = VMEM((3 * C, 3 * C), BF16)
PRODUCT = VMEM((ROWS, 3 * C), F32)


def counts_mem(counts):
    return pltpu.SMEM(counts.shape, jnp.int32)


def run_edge(place, core, counts, g):
    return call(
        edge_kernel,
        (place, core),
        (),
        (counts, g),
        [ONE, ONE, ACT],
        [counts_mem(counts), dma((4,))],
        (0, 600_000),
    )


def run_forward(place, counts, x, gain, shift, wt_t, w_t):
    return call(
        forward_kernel,
        (place,),
        (),
        (counts, x, gain, shift, wt_t, w_t),
        [
            ACT, ACT, array((ROWS - PIX, C), BF16), array((PIX, C), BF16), array((2, 8, C), F32),
            array(wt_t.shape, BF16), ACT,
        ],
        [counts_mem(counts), VECTOR, VECTOR, WEIGHTS, COLUMNS, STACKED, PRODUCT, dma((11,))],
        (2 * ROWS * 9 * C * C, 4_000_000),
    )


def run_own(u, inner, g_own):
    out = array((C, 8 * LANES), F32)
    return call(own_kernel, (), (u, inner, g_own), (), out, [], (2 * ROWS * 3 * C * C, 2_500_000))


def run_grad(place, core, whole, u, last, one, two):
    return call(
        grad_kernel,
        (place, core),
        (whole, u, last, one, two),
        (),
        [array((HALF, LANES), F32), array((HALF, LANES), BF16)],
        [VMEM((C, 8 * LANES), F32)],
        (4 * PIX * C * C, 2_500_000),
    )


def run_temporal(place, core, y, g_own, one, two, wt_own, counts):
    return call(
        temporal_kernel,
        (place, core),
        (y, g_own, one, two, wt_own),
        (counts,),
        ACT,
        [VMEM((5 * PIX, C), BF16), counts_mem(counts), dma((1,))],
        (2 * ROWS * 3 * C * C, 2_500_000),
    )


def run_spatial(place, dy, stats, x, counts, gain, shift, w_t):
    return call(
        spatial_kernel,
        (place,),
        (dy, stats, x),
        (counts, gain, shift, w_t),
        ACT,
        [counts_mem(counts), VECTOR, VECTOR, WEIGHTS, COLUMNS, STACKED, PRODUCT, dma((7,))],
        (2 * ROWS * 9 * C * C, 4_000_000),
    )


def run_sum(parts, copies):
    def body(*refs):
        sum_kernel(copies, *refs)

    out = array((copies,) + parts.shape[1:], BF16)
    return call(body, (), (parts,), (), out, [], (parts.size, 2 * parts.size))


def run_add(core, keep, both):
    out = array(keep.shape, BF16)
    return call(add_kernel, (core,), (keep, both), (), out, [], (keep.size, 8 * keep.size))


def run_final(scale, both):
    def body(*refs):
        final_kernel(scale, *refs)

    whole = VMEM((C, 3 * C), F32)
    out = array((C, 3 * C), F32)
    cost = (1_000_000, 2_000_000)
    return call(body, (), (both,), (), out, [whole, dma((4,))], cost, out_away=True)


def shards(frames_in, cotangent, counts, norm_gain, norm_shift, spatial_weight, temporal_weight):
    shape = frames_in.shape
    x = frames_in.reshape(ROWS, C)
    g = cotangent.reshape(ROWS, C)
    place = lax.axis_index("tm").astype(jnp.int32).reshape(1)
    core = lax.axis_index("c").astype(jnp.int32).reshape(1)
    w_t = spatial_weight.T
    wt_t = temporal_weight.T
    tm_size = lax.axis_size("tm")
    pairs = [[], []]
    for c in range(2):
        for t in range(tm_size - 1):
            here = c * tm_size + t
            pairs[(t + c) % 2] += [(here, here + 1), (here + 1, here)]

    one, two, g_own = run_edge(place, core, counts, g)
    one = lax.ppermute(one, ("c", "tm"), pairs[0])
    two = lax.ppermute(two, ("c", "tm"), pairs[1])
    y, u, inner, last, stats, wt_own, x_own = run_forward(
        place, counts, x, norm_gain, norm_shift, wt_t, w_t
    )
    whole = run_own(u, inner, g_own)
    keep, send = run_grad(place, core, whole, u, last, one, two)

    near, far = groups()
    size = len(near[0])
    part = run_add(core, keep, lax.all_gather(send, "c")).reshape(size, HALF // size, LANES)
    part = run_sum(exchange(part, near), len(far[0]))
    part, one = lax.optimization_barrier((part, one))
    dy = run_temporal(place, core, y, g_own, one, two, wt_own, counts)
    d_in = run_spatial(place, dy, stats, x_own, counts, norm_gain, norm_shift, w_t)
    part, d_in = lax.optimization_barrier((exchange(part, far), d_in))
    part = run_sum(part, size)
    mine = exchange(part, near).reshape(HALF, LANES)
    both = lax.all_gather(mine, "c")

    frames = lax.axis_size(("z", "c")) * 2 * tm_size
    grad = run_final(1.0 / math.sqrt(frames * HH * WW), both)
    return (d_in.reshape(shape), grad.T)


def groups():
    zs, ys, xs = lax.axis_size("z"), lax.axis_size("tm") // X_SIZE, X_SIZE

    def at(z, c, y, x):
        return ((z * 2 + c) * ys + y) * xs + x

    near = [
        [at(z + i, c, y + j, x) for i in range(2) for j in range(2) for x in range(xs)]
        for z in range(0, zs, 2)
        for c in range(2)
        for y in range(0, ys, 2)
    ]
    far = [
        [at(z, c, y, x) for z in range(i, zs, 2) for y in range(j, ys, 2)]
        for i in range(2)
        for j in range(2)
        for c in range(2)
        for x in range(xs)
    ]
    return near, far


def exchange(parts, members):
    return lax.all_to_all(parts, ("z", "c", "tm"), 0, 0, axis_index_groups=members, tiled=True)


def solution(mesh):
    devices = mesh.devices
    dp, tm = devices.shape
    split = Mesh(devices.reshape(dp // 2, 2, tm), ("z", "c", "tm"))
    return jax.shard_map(
        shards,
        mesh=split,
        in_specs=(
            P(("z", "c"), "tm", None, None, None),
            P(("z", "c"), "tm", None, None, None),
            P(("z", "c"), None),
            P(),
            P(),
            P(),
            P(),
        ),
        out_specs=(P(("z", "c"), "tm", None, None, None), P()),
        check_vma=False,
    )
```

```python
import math

import jax
import jax.numpy as jnp
from jax import lax
from jax.experimental import pallas as pl
from jax.experimental.pallas import tpu as pltpu
from jax.sharding import Mesh
from jax.sharding import PartitionSpec as P

F32 = jnp.float32
BF16 = jnp.bfloat16
C = 320
GROUPS = 32
PER_GROUP = C // GROUPS
CAP = 3
HH = 32
WW = 8
PIX = HH * WW
ROWS = CAP * PIX
ENTRIES = PIX * PER_GROUP
VMEM = pltpu.VMEM
LANES = 128
X_SIZE = 4
HALF = 4 * C
PARAMS = pltpu.CompilerParams(vmem_limit_bytes=28 * 1024 * 1024)


def group_matrix():
    row = lax.broadcasted_iota(jnp.int32, (C, C), 0).astype(F32)
    col = lax.broadcasted_iota(jnp.int32, (C, C), 1).astype(F32)
    inv = 1.0 / PER_GROUP
    same = jnp.floor((row + 0.5) * inv) == jnp.floor((col + 0.5) * inv)
    return same.astype(F32).astype(BF16)


def group_mean(sums, matrix):
    high = sums.astype(BF16).astype(F32)
    rest = sums - high
    middle = rest.astype(BF16).astype(F32)
    terms = jnp.concatenate([high, middle, rest - middle, jnp.zeros((8, C), F32)], axis=0)
    added = jnp.dot(terms.astype(BF16), matrix, preferred_element_type=F32)
    return (added[0:8] + added[8:16] + added[16:24]) / ENTRIES


def frame(s):
    if isinstance(s, int):
        return pl.ds(s * PIX, PIX)
    return pl.ds(pl.multiple_of(s * PIX, PIX), PIX)


def sigmoid(values):
    return 0.5 * jnp.tanh(0.5 * values) + 0.5


def shifted(values, step):
    cube = values.reshape(HH, WW, C)
    rolled = jnp.roll(cube, -step, axis=1)
    col = lax.broadcasted_iota(jnp.int32, (HH, WW, C), 1)
    keep = (col < WW - 1) if step > 0 else (col > 0)
    return jnp.where(keep, rolled, 0.0).reshape(PIX, C)


def down(values):
    return jnp.concatenate([jnp.zeros((WW, C), F32), values[:-WW]], axis=0)


def up(values):
    return jnp.concatenate([values[WW:], jnp.zeros((WW, C), F32)], axis=0)


def start_all(sems, *pairs):
    copies = [pltpu.make_async_copy(src, dst, sems.at[i]) for i, (src, dst) in enumerate(pairs)]
    for copy in copies:
        copy.start()
    return copies


def packed(values):
    half = PIX // 2
    rest = values[:, 2 * LANES :]
    rest = jnp.concatenate([rest[:half], rest[half:]], axis=1)
    return jnp.concatenate([values[:, :LANES], values[:, LANES : 2 * LANES], rest], axis=0)


def unpacked(values):
    rest = values[2 * PIX :, :]
    tail = C - 2 * LANES
    rest = jnp.concatenate([rest[:, :tail], rest[:, tail:]], axis=0)
    return jnp.concatenate([values[:PIX], values[PIX : 2 * PIX], rest], axis=1)


def left_first(t_ref, core_ref):
    return lax.rem(t_ref[0] + core_ref[0], 2)


def edge_kernel(
    t_ref, core_ref, counts_hbm, g_hbm, one_ref, two_ref, g_ref, counts, sems
):
    frames = [(g_hbm.at[frame(s), :], g_ref.at[frame(s), :]) for s in range(CAP)]
    for copy in start_all(sems, (counts_hbm, counts), *frames):
        copy.wait()
    last = counts[0, t_ref[0]] - 1
    turn = left_first(t_ref, core_ref)
    one_ref[...] = packed(g_ref[frame(last * (1 - turn)), :])
    two_ref[...] = packed(g_ref[frame(last * turn), :])


def forward_kernel(
    t_ref, g_ref, counts_hbm, x_hbm, gain_hbm, shift_hbm, wt_hbm, w_hbm, y_ref, u_ref, whole_ref,
    last_ref, stats_ref, wt_ref, x_ref, inner, flipped, counts, gain_ref, shift_ref, w_ref, cols, wst, prod, sems,
):
    weights = [(w_hbm.at[pl.ds(q, 80), :], w_ref.at[pl.ds(q, 80), :]) for q in range(0, C, 80)]
    frames = [(x_hbm.at[frame(s), :], x_ref.at[frame(s), :]) for s in range(CAP)]
    copies = start_all(
        sems,
        *frames,
        (gain_hbm, gain_ref),
        (shift_hbm, shift_ref),
        (counts_hbm, counts),
        *weights,
        (wt_hbm, wt_ref),
    )
    matrix = group_matrix()
    blank = jnp.zeros((8 - CAP, C), F32)

    def per_frame(fn):
        return jnp.concatenate([fn(s) for s in range(CAP)] + [blank], axis=0)

    flipped[...] = g_ref[...].T
    edge = 3 * C - 3 * C % LANES
    whole_ref[:, edge:] = jnp.zeros((C, 8 * LANES - edge), F32)
    for copy in copies[:CAP]:
        copy.wait()

    def load(s):
        return x_ref[s * PIX : (s + 1) * PIX, :].astype(F32)

    mean = group_mean(per_frame(lambda s: jnp.sum(load(s), axis=0, keepdims=True)), matrix)

    def squares(s):
        centred = load(s) - mean[s : s + 1]
        return jnp.sum(centred * centred, axis=0, keepdims=True)

    inv = lax.rsqrt(group_mean(per_frame(squares), matrix) + 1e-05)
    stats_ref[0] = mean
    stats_ref[1] = inv
    for copy in copies[CAP : CAP + 3]:
        copy.wait()
    n = counts[0, t_ref[0]]
    gain = gain_ref[...].reshape(1, C)
    shift = shift_ref[...].reshape(1, C)

    def activate(s):
        values = (x_ref[frame(s), :].astype(F32) - stats_ref[0, pl.ds(s, 1), :]) * stats_ref[
            1, pl.ds(s, 1), :
        ] * gain + shift
        act = values * sigmoid(values)
        cols[frame(s), 0:C] = shifted(act, -1).astype(BF16)
        cols[frame(s), C : 2 * C] = act.astype(BF16)
        cols[frame(s), 2 * C : 3 * C] = shifted(act, 1).astype(BF16)

    for s in range(CAP):
        activate(s)
    for copy in copies[CAP + 3 : -1]:
        copy.wait()
    for i in range(3):
        wst[i * C : (i + 1) * C, :] = w_ref[:, i * 3 * C : (i + 1) * 3 * C]
    prod[...] = lax.dot_general(
        cols[...], wst[...], (((1,), (1,)), ((), ())), preferred_element_type=F32
    )

    zero = jnp.zeros((PIX, C), BF16)

    def add(s):
        rows = frame(s)
        mixed = down(prod[rows, 0:C]) + prod[rows, C : 2 * C] + up(prod[rows, 2 * C : 3 * C])
        y = (x_ref[rows, :].astype(F32) + mixed).astype(BF16)
        y_ref[rows, :] = y
        yf = y.astype(F32)
        units = (yf * sigmoid(yf)).astype(BF16)
        u_ref[rows, :] = jnp.where(jnp.int32(s) < n, units, zero)
        if s < CAP - 1:
            inner[rows, :] = jnp.where(jnp.int32(s + 1) < n, units, zero)

    for s in range(CAP):
        add(s)
    last_ref[...] = u_ref[frame(n - 1), :]

    def term(own, taken):
        return jnp.dot(own, taken, preferred_element_type=F32)

    whole_ref[:, 0:C] = term(flipped[:, PIX:], inner[...])
    whole_ref[:, C : 2 * C] = term(flipped[...], u_ref[...])
    whole_ref[:, 2 * C : 3 * C] = term(flipped[:, 0 : ROWS - PIX], u_ref[PIX:, :])
    copies[-1].wait()


def sides(turn, one_ref, two_ref):
    before = jnp.where(turn == 1, one_ref[...], two_ref[...])
    after = jnp.where(turn == 1, two_ref[...], one_ref[...])
    return unpacked(before), unpacked(after)


def grad_kernel(
    t_ref, core_ref, whole_ref, u_ref, last_ref, one_ref, two_ref, keep_ref, send_ref, whole
):
    core = core_ref[0]
    before, after = sides(left_first(t_ref, core_ref), one_ref, two_ref)
    whole[...] = whole_ref[...]
    whole[:, 0:C] += jnp.dot(after.T, last_ref[...], preferred_element_type=F32)
    whole[:, 2 * C : 3 * C] += jnp.dot(before.T, u_ref[0:PIX, :], preferred_element_type=F32)
    for j in range(4):
        first = whole[:, j * LANES : (j + 1) * LANES]
        second = whole[:, (j + 4) * LANES : (j + 5) * LANES]
        keep_ref[j * C : (j + 1) * C, :] = jnp.where(core == 0, first, second)
        send_ref[j * C : (j + 1) * C, :] = jnp.where(core == 0, second, first).astype(BF16)


def backward_kernel(
    t_ref, core_ref, y_ref, g_ref, one_ref, two_ref, wt_ref, stats_ref, x_ref, counts_hbm, gain_hbm,
    shift_hbm, w_hbm, out_ref, ext, dys, counts, gain_ref, shift_ref, w_ref, cols, wst, prod, sems,
):
    weights = [(w_hbm.at[pl.ds(q, 80), :], w_ref.at[pl.ds(q, 80), :]) for q in range(0, C, 80)]
    copies = start_all(
        sems,
        (counts_hbm, counts),
        *weights,
        (gain_hbm, gain_ref),
        (shift_hbm, shift_ref),
    )
    before, after = sides(left_first(t_ref, core_ref), one_ref, two_ref)
    ext[0:PIX, :] = before
    ext[PIX : PIX + ROWS, :] = g_ref[...]
    ext[PIX + ROWS :, :] = after
    copies[0].wait()
    n = counts[0, t_ref[0]]
    ext[frame(n + 1), :] = after
    for s in range(CAP):
        back = jnp.zeros((PIX, C), F32)
        for k in range(3):
            back = back + jnp.dot(
                ext[frame(s + 2 - k), :],
                wt_ref[:, k * C : (k + 1) * C],
                preferred_element_type=F32,
            )
        yf = y_ref[frame(s), :].astype(F32)
        sig = sigmoid(yf)
        back = (sig * (1.0 + yf * (1.0 - sig)) * back).astype(BF16)
        dy = (g_ref[frame(s), :].astype(F32) + back.astype(F32)).astype(BF16)
        dys[frame(s), :] = dy
        dyf = dy.astype(F32)
        cols[frame(s), 0:C] = shifted(dyf, 1).astype(BF16)
        cols[frame(s), C : 2 * C] = dy
        cols[frame(s), 2 * C : 3 * C] = shifted(dyf, -1).astype(BF16)
    for copy in copies[1:]:
        copy.wait()
    for i in range(3):
        for j in range(3):
            tap = 3 * i + j
            wst[j * C : (j + 1) * C, i * C : (i + 1) * C] = w_ref[:, tap * C : (tap + 1) * C]
    prod[...] = jnp.dot(cols[...], wst[...], preferred_element_type=F32)
    matrix = group_matrix()
    gain = gain_ref[...].reshape(1, C)
    shift = shift_ref[...].reshape(1, C)

    def finish(s):
        rows = frame(s)
        da = up(prod[rows, 0:C]) + prod[rows, C : 2 * C] + down(prod[rows, 2 * C : 3 * C])
        mean = stats_ref[0, pl.ds(s, 1), :]
        inv = stats_ref[1, pl.ds(s, 1), :]
        normed = (x_ref[rows, :].astype(F32) - mean) * inv
        values = normed * gain + shift
        sig = sigmoid(values)
        dn = da * (sig * (1.0 + values * (1.0 - sig))) * gain
        sums = jnp.concatenate(
            [
                jnp.sum(dn, axis=0, keepdims=True),
                jnp.sum(dn * normed, axis=0, keepdims=True),
                jnp.zeros((6, C), F32),
            ],
            axis=0,
        )
        means = group_mean(sums, matrix)
        dx = inv * (dn - means[0:1] - normed * means[1:2])
        total = dys[rows, :].astype(F32) + dx
        out_ref[rows, :] = jnp.where(jnp.int32(s) < n, total, 0.0).astype(BF16)

    for s in range(CAP):
        finish(s)


def add_kernel(core_ref, keep_ref, both_ref, out_ref):
    got = jnp.where(core_ref[0] == 0, both_ref[1], both_ref[0])
    out_ref[...] = (keep_ref[...] + got.astype(F32)).astype(BF16)


def sum_kernel(copies, x_ref, out_ref):
    total = x_ref[0].astype(F32)
    for i in range(1, x_ref.shape[0]):
        total = total + x_ref[i].astype(F32)
    total = total.astype(BF16)
    for i in range(copies):
        out_ref[i] = total


def final_kernel(scale, both_ref, out_hbm, whole, sems):
    copies = []
    for i, row in enumerate(range(0, C, C // 4)):
        rows = pl.ds(row, C // 4)
        for j in range(8):
            width = min(LANES, 3 * C - j * LANES)
            start = (j % 4) * C + row
            part = both_ref[j // 4, start : start + C // 4, :].astype(F32) * scale
            whole[rows, j * LANES : j * LANES + width] = part[:, :width]
        copies.append(pltpu.make_async_copy(whole.at[rows, :], out_hbm.at[rows, :], sems.at[i]))
        copies[-1].start()
    for copy in copies:
        copy.wait()


SMEM_SPEC = pl.BlockSpec(memory_space=pltpu.SMEM)
VMEM_SPEC = pl.BlockSpec(memory_space=pltpu.VMEM)
HBM_SPEC = pl.BlockSpec(memory_space=pltpu.HBM)


def call(body, scalars, arrays, away, outs, scratch, cost, out_away=False):
    away = [pltpu.with_memory_space_constraint(a, pltpu.HBM) for a in away]
    out_spec = HBM_SPEC if out_away else VMEM_SPEC
    return pl.pallas_call(
        body,
        out_shape=outs,
        in_specs=[SMEM_SPEC] * len(scalars) + [VMEM_SPEC] * len(arrays) + [HBM_SPEC] * len(away),
        out_specs=[VMEM_SPEC] * len(outs) if isinstance(outs, list) else out_spec,
        scratch_shapes=scratch,
        compiler_params=PARAMS,
        cost_estimate=pl.CostEstimate(flops=cost[0], bytes_accessed=cost[1], transcendentals=0),
    )(*scalars, *arrays, *away)


array = jax.ShapeDtypeStruct
dma = pltpu.SemaphoreType.DMA
ACT = array((ROWS, C), BF16)
ONE = array((PIX * C // LANES, LANES), BF16)
VECTOR = VMEM((C,), F32)
WEIGHTS = VMEM((C, 9 * C), BF16)
COLUMNS = VMEM((ROWS, 3 * C), BF16)
STACKED = VMEM((3 * C, 3 * C), BF16)
PRODUCT = VMEM((ROWS, 3 * C), F32)


def counts_mem(counts):
    return pltpu.SMEM(counts.shape, jnp.int32)


def run_edge(place, core, counts, g):
    return call(
        edge_kernel,
        (place, core),
        (),
        (counts, g),
        [ONE, ONE, ACT],
        [counts_mem(counts), dma((4,))],
        (0, 600_000),
    )


def run_forward(place, g_own, counts, x, gain, shift, wt_t, w_t):
    return call(
        forward_kernel,
        (place,),
        (g_own,),
        (counts, x, gain, shift, wt_t, w_t),
        [
            ACT, ACT, array((C, 8 * LANES), F32), array((PIX, C), BF16), array((2, 8, C), F32),
            array(wt_t.shape, BF16), ACT,
        ],
        [
            VMEM((ROWS - PIX, C), BF16), VMEM((C, ROWS), BF16), counts_mem(counts), VECTOR, VECTOR,
            WEIGHTS, COLUMNS, STACKED, PRODUCT, dma((11,)),
        ],
        (2 * ROWS * 12 * C * C, 4_000_000),
    )


def run_grad(place, core, whole, u, last, one, two):
    return call(
        grad_kernel,
        (place, core),
        (whole, u, last, one, two),
        (),
        [array((HALF, LANES), F32), array((HALF, LANES), BF16)],
        [VMEM((C, 8 * LANES), F32)],
        (4 * PIX * C * C, 2_500_000),
    )


def run_backward(place, core, y, g_own, one, two, wt_own, stats, x_own, counts, gain, shift, w_t):
    return call(
        backward_kernel,
        (place, core),
        (y, g_own, one, two, wt_own, stats, x_own),
        (counts, gain, shift, w_t),
        ACT,
        [
            VMEM((5 * PIX, C), BF16), VMEM((ROWS, C), BF16), counts_mem(counts), VECTOR, VECTOR,
            WEIGHTS, COLUMNS, STACKED, PRODUCT, dma((7,)),
        ],
        (2 * ROWS * 12 * C * C, 4_000_000),
    )


def run_sum(parts, copies):
    def body(*refs):
        sum_kernel(copies, *refs)

    out = array((copies,) + parts.shape[1:], BF16)
    return call(body, (), (parts,), (), out, [], (parts.size, 2 * parts.size))


def run_add(core, keep, both):
    out = array(keep.shape, BF16)
    return call(add_kernel, (core,), (keep, both), (), out, [], (keep.size, 8 * keep.size))


def run_final(scale, both):
    def body(*refs):
        final_kernel(scale, *refs)

    whole = VMEM((C, 3 * C), F32)
    out = array((C, 3 * C), F32)
    cost = (1_000_000, 2_000_000)
    return call(body, (), (both,), (), out, [whole, dma((4,))], cost, out_away=True)


def shards(frames_in, cotangent, counts, norm_gain, norm_shift, spatial_weight, temporal_weight):
    shape = frames_in.shape
    x = frames_in.reshape(ROWS, C)
    g = cotangent.reshape(ROWS, C)
    place = lax.axis_index("tm").astype(jnp.int32).reshape(1)
    core = lax.axis_index("c").astype(jnp.int32).reshape(1)
    w_t = spatial_weight.T
    wt_t = temporal_weight.T
    tm_size = lax.axis_size("tm")
    pairs = [[], []]
    for c in range(2):
        for t in range(tm_size - 1):
            here = c * tm_size + t
            pairs[(t + c) % 2] += [(here, here + 1), (here + 1, here)]

    one, two, g_own = run_edge(place, core, counts, g)
    one = lax.ppermute(one, ("c", "tm"), pairs[0])
    two = lax.ppermute(two, ("c", "tm"), pairs[1])
    y, u, whole, last, stats, wt_own, x_own = run_forward(
        place, g_own, counts, x, norm_gain, norm_shift, wt_t, w_t
    )
    keep, send = run_grad(place, core, whole, u, last, one, two)

    near, far = groups()
    size = len(near[0])
    part = run_add(core, keep, lax.all_gather(send, "c")).reshape(size, HALF // size, LANES)
    part = run_sum(exchange(part, near), len(far[0]))
    part, one = lax.optimization_barrier((part, one))
    d_in = run_backward(
        place, core, y, g_own, one, two, wt_own, stats, x_own, counts, norm_gain, norm_shift, w_t
    )
    part, d_in = lax.optimization_barrier((exchange(part, far), d_in))
    part = run_sum(part, size)
    mine = exchange(part, near).reshape(HALF, LANES)
    both = lax.all_gather(mine, "c")

    frames = lax.axis_size(("z", "c")) * 2 * tm_size
    grad = run_final(1.0 / math.sqrt(frames * HH * WW), both)
    return (d_in.reshape(shape), grad.T)


def groups():
    zs, ys, xs = lax.axis_size("z"), lax.axis_size("tm") // X_SIZE, X_SIZE

    def at(z, c, y, x):
        return ((z * 2 + c) * ys + y) * xs + x

    def kind(i):
        return bin(i).count("1") % 2

    def pair(i):
        return sorted((i, i + 1), key=kind)

    def alike(i, size):
        return [p for p in range(size) if kind(p) == i]

    near = [
        [at(zz, c, yy, x) for zz in pair(z) for yy in pair(y) for x in range(xs)]
        for z in range(0, zs, 2)
        for c in range(2)
        for y in range(0, ys, 2)
    ]
    far = [
        [at(z, c, y, x) for z in alike(i, zs) for y in alike(j, ys)]
        for i in range(2)
        for j in range(2)
        for c in range(2)
        for x in range(xs)
    ]
    return near, far


def exchange(parts, members):
    return lax.all_to_all(parts, ("z", "c", "tm"), 0, 0, axis_index_groups=members, tiled=True)


def solution(mesh):
    devices = mesh.devices
    dp, tm = devices.shape
    split = Mesh(devices.reshape(dp // 2, 2, tm), ("z", "c", "tm"))
    return jax.shard_map(
        shards,
        mesh=split,
        in_specs=(
            P(("z", "c"), "tm", None, None, None),
            P(("z", "c"), "tm", None, None, None),
            P(("z", "c"), None),
            P(),
            P(),
            P(),
            P(),
        ),
        out_specs=(P(("z", "c"), "tm", None, None, None), P()),
        check_vma=False,
    )
```

```python
import math

import jax
import jax.numpy as jnp
from jax import lax
from jax.experimental import pallas as pl
from jax.experimental.pallas import tpu as pltpu
from jax.sharding import Mesh
from jax.sharding import PartitionSpec as P

F32 = jnp.float32
BF16 = jnp.bfloat16
C = 320
GROUPS = 32
PER_GROUP = C // GROUPS
CAP = 3
HH = 32
WW = 8
PIX = HH * WW
ROWS = CAP * PIX
ENTRIES = PIX * PER_GROUP
VMEM = pltpu.VMEM
LANES = 128
X_SIZE = 4
HALF = 4 * C
PARAMS = pltpu.CompilerParams(vmem_limit_bytes=28 * 1024 * 1024)


def group_matrix():
    row = lax.broadcasted_iota(jnp.int32, (C, C), 0).astype(F32)
    col = lax.broadcasted_iota(jnp.int32, (C, C), 1).astype(F32)
    inv = 1.0 / PER_GROUP
    same = jnp.floor((row + 0.5) * inv) == jnp.floor((col + 0.5) * inv)
    return same.astype(F32).astype(BF16)


def group_mean(sums, matrix):
    high = sums.astype(BF16).astype(F32)
    rest = sums - high
    middle = rest.astype(BF16).astype(F32)
    terms = jnp.concatenate([high, middle, rest - middle, jnp.zeros((8, C), F32)], axis=0)
    added = jnp.dot(terms.astype(BF16), matrix, preferred_element_type=F32)
    return (added[0:8] + added[8:16] + added[16:24]) / ENTRIES


def frame(s):
    if isinstance(s, int):
        return pl.ds(s * PIX, PIX)
    return pl.ds(pl.multiple_of(s * PIX, PIX), PIX)


def sigmoid(values):
    return 0.5 * jnp.tanh(0.5 * values) + 0.5


def shifted(values, step):
    cube = values.reshape(HH, WW, C)
    rolled = jnp.roll(cube, -step, axis=1)
    col = lax.broadcasted_iota(jnp.int32, (HH, WW, C), 1)
    keep = (col < WW - 1) if step > 0 else (col > 0)
    return jnp.where(keep, rolled, 0.0).reshape(PIX, C)


def down(values):
    return jnp.concatenate([jnp.zeros((WW, C), F32), values[:-WW]], axis=0)


def up(values):
    return jnp.concatenate([values[WW:], jnp.zeros((WW, C), F32)], axis=0)


def start_all(sems, *pairs):
    copies = [pltpu.make_async_copy(src, dst, sems.at[i]) for i, (src, dst) in enumerate(pairs)]
    for copy in copies:
        copy.start()
    return copies


def packed(values):
    half = PIX // 2
    rest = values[:, 2 * LANES :]
    rest = jnp.concatenate([rest[:half], rest[half:]], axis=1)
    return jnp.concatenate([values[:, :LANES], values[:, LANES : 2 * LANES], rest], axis=0)


def unpacked(values):
    rest = values[2 * PIX :, :]
    tail = C - 2 * LANES
    rest = jnp.concatenate([rest[:, :tail], rest[:, tail:]], axis=0)
    return jnp.concatenate([values[:PIX], values[PIX : 2 * PIX], rest], axis=1)


def left_first(t_ref, core_ref):
    return lax.rem(t_ref[0] + core_ref[0], 2)


def edge_kernel(
    t_ref, core_ref, counts_hbm, g_hbm, one_ref, two_ref, g_ref, counts, sems
):
    frames = [(g_hbm.at[frame(s), :], g_ref.at[frame(s), :]) for s in range(CAP)]
    for copy in start_all(sems, (counts_hbm, counts), *frames):
        copy.wait()
    last = counts[0, t_ref[0]] - 1
    turn = left_first(t_ref, core_ref)
    one_ref[...] = packed(g_ref[frame(last * (1 - turn)), :])
    two_ref[...] = packed(g_ref[frame(last * turn), :])


def forward_kernel(
    t_ref, g_ref, counts_hbm, x_hbm, gain_hbm, shift_hbm, wt_hbm, w_hbm, y_ref, u_ref, whole_ref,
    last_ref, stats_ref, wt_ref, x_ref, inner, flipped, counts, gain_ref, shift_ref, w_ref, cols, wst, prod, sems,
):
    weights = [(w_hbm.at[pl.ds(q, 80), :], w_ref.at[pl.ds(q, 80), :]) for q in range(0, C, 80)]
    frames = [(x_hbm.at[frame(s), :], x_ref.at[frame(s), :]) for s in range(CAP)]
    copies = start_all(
        sems,
        *frames,
        (gain_hbm, gain_ref),
        (shift_hbm, shift_ref),
        (counts_hbm, counts),
        *weights,
        (wt_hbm, wt_ref),
    )
    matrix = group_matrix()
    blank = jnp.zeros((8 - CAP, C), F32)

    def per_frame(fn):
        return jnp.concatenate([fn(s) for s in range(CAP)] + [blank], axis=0)

    flipped[...] = g_ref[...].T
    edge = 3 * C - 3 * C % LANES
    whole_ref[:, edge:] = jnp.zeros((C, 8 * LANES - edge), F32)
    for copy in copies[:CAP]:
        copy.wait()

    def load(s):
        return x_ref[s * PIX : (s + 1) * PIX, :].astype(F32)

    mean = group_mean(per_frame(lambda s: jnp.sum(load(s), axis=0, keepdims=True)), matrix)

    def squares(s):
        centred = load(s) - mean[s : s + 1]
        return jnp.sum(centred * centred, axis=0, keepdims=True)

    inv = lax.rsqrt(group_mean(per_frame(squares), matrix) + 1e-05)
    stats_ref[0] = mean
    stats_ref[1] = inv
    for copy in copies[CAP : CAP + 3]:
        copy.wait()
    n = counts[0, t_ref[0]]
    gain = gain_ref[...].reshape(1, C)
    shift = shift_ref[...].reshape(1, C)

    def activate(s):
        values = (x_ref[frame(s), :].astype(F32) - stats_ref[0, pl.ds(s, 1), :]) * stats_ref[
            1, pl.ds(s, 1), :
        ] * gain + shift
        act = values * sigmoid(values)
        cols[frame(s), 0:C] = shifted(act, -1).astype(BF16)
        cols[frame(s), C : 2 * C] = act.astype(BF16)
        cols[frame(s), 2 * C : 3 * C] = shifted(act, 1).astype(BF16)

    for s in range(CAP):
        activate(s)
    for copy in copies[CAP + 3 : -1]:
        copy.wait()
    for i in range(3):
        wst[i * C : (i + 1) * C, :] = w_ref[:, i * 3 * C : (i + 1) * 3 * C]
    prod[...] = lax.dot_general(
        cols[...], wst[...], (((1,), (1,)), ((), ())), preferred_element_type=F32
    )

    zero = jnp.zeros((PIX, C), BF16)

    def add(s):
        rows = frame(s)
        mixed = down(prod[rows, 0:C]) + prod[rows, C : 2 * C] + up(prod[rows, 2 * C : 3 * C])
        y = (x_ref[rows, :].astype(F32) + mixed).astype(BF16)
        y_ref[rows, :] = y
        yf = y.astype(F32)
        units = (yf * sigmoid(yf)).astype(BF16)
        u_ref[rows, :] = jnp.where(jnp.int32(s) < n, units, zero)
        if s < CAP - 1:
            inner[rows, :] = jnp.where(jnp.int32(s + 1) < n, units, zero)

    for s in range(CAP):
        add(s)
    last_ref[...] = u_ref[frame(n - 1), :]

    def term(own, taken):
        return jnp.dot(own, taken, preferred_element_type=F32)

    whole_ref[:, 0:C] = term(flipped[:, PIX:], inner[...])
    whole_ref[:, C : 2 * C] = term(flipped[...], u_ref[...])
    whole_ref[:, 2 * C : 3 * C] = term(flipped[:, 0 : ROWS - PIX], u_ref[PIX:, :])
    copies[-1].wait()


def sides(turn, one_ref, two_ref):
    before = jnp.where(turn == 1, one_ref[...], two_ref[...])
    after = jnp.where(turn == 1, two_ref[...], one_ref[...])
    return unpacked(before), unpacked(after)


def grad_kernel(
    t_ref, core_ref, whole_ref, u_ref, last_ref, one_ref, two_ref, keep_ref, send_ref, whole
):
    core = core_ref[0]
    before, after = sides(left_first(t_ref, core_ref), one_ref, two_ref)
    whole[...] = whole_ref[...]
    whole[:, 0:C] += jnp.dot(after.T, last_ref[...], preferred_element_type=F32)
    whole[:, 2 * C : 3 * C] += jnp.dot(before.T, u_ref[0:PIX, :], preferred_element_type=F32)
    for j in range(4):
        first = whole[:, j * LANES : (j + 1) * LANES]
        second = whole[:, (j + 4) * LANES : (j + 5) * LANES]
        keep_ref[j * C : (j + 1) * C, :] = jnp.where(core == 0, first, second)
        send_ref[j * C : (j + 1) * C, :] = jnp.where(core == 0, second, first).astype(BF16)


def backward_kernel(
    t_ref, core_ref, y_ref, g_ref, one_ref, two_ref, wt_ref, stats_ref, x_ref, counts_hbm, gain_hbm,
    shift_hbm, w_hbm, out_ref, ext, dys, counts, gain_ref, shift_ref, w_ref, cols, wst, prod, sems,
):
    weights = [(w_hbm.at[pl.ds(q, 80), :], w_ref.at[pl.ds(q, 80), :]) for q in range(0, C, 80)]
    copies = start_all(
        sems,
        (counts_hbm, counts),
        *weights,
        (gain_hbm, gain_ref),
        (shift_hbm, shift_ref),
    )
    before, after = sides(left_first(t_ref, core_ref), one_ref, two_ref)
    ext[0:PIX, :] = before
    ext[PIX : PIX + ROWS, :] = g_ref[...]
    ext[PIX + ROWS :, :] = after
    copies[0].wait()
    n = counts[0, t_ref[0]]
    ext[frame(n + 1), :] = after
    for s in range(CAP):
        back = jnp.zeros((PIX, C), F32)
        for k in range(3):
            back = back + jnp.dot(
                ext[frame(s + 2 - k), :],
                wt_ref[:, k * C : (k + 1) * C],
                preferred_element_type=F32,
            )
        yf = y_ref[frame(s), :].astype(F32)
        sig = sigmoid(yf)
        back = (sig * (1.0 + yf * (1.0 - sig)) * back).astype(BF16)
        dy = (g_ref[frame(s), :].astype(F32) + back.astype(F32)).astype(BF16)
        dys[frame(s), :] = dy
        dyf = dy.astype(F32)
        cols[frame(s), 0:C] = shifted(dyf, 1).astype(BF16)
        cols[frame(s), C : 2 * C] = dy
        cols[frame(s), 2 * C : 3 * C] = shifted(dyf, -1).astype(BF16)
    for copy in copies[1:]:
        copy.wait()
    for i in range(3):
        for j in range(3):
            tap = 3 * i + j
            wst[j * C : (j + 1) * C, i * C : (i + 1) * C] = w_ref[:, tap * C : (tap + 1) * C]
    prod[...] = jnp.dot(cols[...], wst[...], preferred_element_type=F32)
    matrix = group_matrix()
    gain = gain_ref[...].reshape(1, C)
    shift = shift_ref[...].reshape(1, C)

    def finish(s):
        rows = frame(s)
        da = up(prod[rows, 0:C]) + prod[rows, C : 2 * C] + down(prod[rows, 2 * C : 3 * C])
        mean = stats_ref[0, pl.ds(s, 1), :]
        inv = stats_ref[1, pl.ds(s, 1), :]
        normed = (x_ref[rows, :].astype(F32) - mean) * inv
        values = normed * gain + shift
        sig = sigmoid(values)
        dn = da * (sig * (1.0 + values * (1.0 - sig))) * gain
        sums = jnp.concatenate(
            [
                jnp.sum(dn, axis=0, keepdims=True),
                jnp.sum(dn * normed, axis=0, keepdims=True),
                jnp.zeros((6, C), F32),
            ],
            axis=0,
        )
        means = group_mean(sums, matrix)
        dx = inv * (dn - means[0:1] - normed * means[1:2])
        total = dys[rows, :].astype(F32) + dx
        out_ref[rows, :] = jnp.where(jnp.int32(s) < n, total, 0.0).astype(BF16)

    for s in range(CAP):
        finish(s)


def add_kernel(core_ref, keep_ref, both_ref, out_ref):
    got = jnp.where(core_ref[0] == 0, both_ref[1], both_ref[0])
    out_ref[...] = (keep_ref[...] + got.astype(F32)).astype(BF16)


def sum_kernel(copies, x_ref, out_ref):
    total = x_ref[0].astype(F32)
    for i in range(1, x_ref.shape[0]):
        total = total + x_ref[i].astype(F32)
    total = total.astype(BF16)
    for i in range(copies):
        out_ref[i] = total


def final_kernel(scale, both_ref, out_hbm, whole, sems):
    copies = []
    for i, row in enumerate(range(0, C, C // 4)):
        rows = pl.ds(row, C // 4)
        for j in range(8):
            width = min(LANES, 3 * C - j * LANES)
            start = (j % 4) * C + row
            part = both_ref[j // 4, start : start + C // 4, :].astype(F32) * scale
            whole[rows, j * LANES : j * LANES + width] = part[:, :width]
        copies.append(pltpu.make_async_copy(whole.at[rows, :], out_hbm.at[rows, :], sems.at[i]))
        copies[-1].start()
    for copy in copies:
        copy.wait()


SMEM_SPEC = pl.BlockSpec(memory_space=pltpu.SMEM)
VMEM_SPEC = pl.BlockSpec(memory_space=pltpu.VMEM)
HBM_SPEC = pl.BlockSpec(memory_space=pltpu.HBM)


def call(body, scalars, arrays, away, outs, scratch, cost, out_away=False):
    away = [pltpu.with_memory_space_constraint(a, pltpu.HBM) for a in away]
    out_spec = HBM_SPEC if out_away else VMEM_SPEC
    return pl.pallas_call(
        body,
        out_shape=outs,
        in_specs=[SMEM_SPEC] * len(scalars) + [VMEM_SPEC] * len(arrays) + [HBM_SPEC] * len(away),
        out_specs=[VMEM_SPEC] * len(outs) if isinstance(outs, list) else out_spec,
        scratch_shapes=scratch,
        compiler_params=PARAMS,
        cost_estimate=pl.CostEstimate(flops=cost[0], bytes_accessed=cost[1], transcendentals=0),
    )(*scalars, *arrays, *away)


array = jax.ShapeDtypeStruct
dma = pltpu.SemaphoreType.DMA
ACT = array((ROWS, C), BF16)
ONE = array((PIX * C // LANES, LANES), BF16)
VECTOR = VMEM((C,), F32)
WEIGHTS = VMEM((C, 9 * C), BF16)
COLUMNS = VMEM((ROWS, 3 * C), BF16)
STACKED = VMEM((3 * C, 3 * C), BF16)
PRODUCT = VMEM((ROWS, 3 * C), F32)


def counts_mem(counts):
    return pltpu.SMEM(counts.shape, jnp.int32)


def run_edge(place, core, counts, g):
    return call(
        edge_kernel,
        (place, core),
        (),
        (counts, g),
        [ONE, ONE, ACT],
        [counts_mem(counts), dma((4,))],
        (0, 600_000),
    )


def run_forward(place, g_own, counts, x, gain, shift, wt_t, w_t):
    return call(
        forward_kernel,
        (place,),
        (g_own,),
        (counts, x, gain, shift, wt_t, w_t),
        [
            ACT, ACT, array((C, 8 * LANES), F32), array((PIX, C), BF16), array((2, 8, C), F32),
            array(wt_t.shape, BF16), ACT,
        ],
        [
            VMEM((ROWS - PIX, C), BF16), VMEM((C, ROWS), BF16), counts_mem(counts), VECTOR, VECTOR,
            WEIGHTS, COLUMNS, STACKED, PRODUCT, dma((11,)),
        ],
        (2 * ROWS * 12 * C * C, 4_000_000),
    )


def run_grad(place, core, whole, u, last, one, two):
    return call(
        grad_kernel,
        (place, core),
        (whole, u, last, one, two),
        (),
        [array((HALF, LANES), F32), array((HALF, LANES), BF16)],
        [VMEM((C, 8 * LANES), F32)],
        (4 * PIX * C * C, 2_500_000),
    )


def run_backward(place, core, y, g_own, one, two, wt_own, stats, x_own, counts, gain, shift, w_t):
    return call(
        backward_kernel,
        (place, core),
        (y, g_own, one, two, wt_own, stats, x_own),
        (counts, gain, shift, w_t),
        ACT,
        [
            VMEM((5 * PIX, C), BF16), VMEM((ROWS, C), BF16), counts_mem(counts), VECTOR, VECTOR,
            WEIGHTS, COLUMNS, STACKED, PRODUCT, dma((7,)),
        ],
        (2 * ROWS * 12 * C * C, 4_000_000),
    )


def run_sum(parts, copies):
    def body(*refs):
        sum_kernel(copies, *refs)

    out = array((copies,) + parts.shape[1:], BF16)
    return call(body, (), (parts,), (), out, [], (parts.size, 2 * parts.size))


def run_add(core, keep, both):
    out = array(keep.shape, BF16)
    return call(add_kernel, (core,), (keep, both), (), out, [], (keep.size, 8 * keep.size))


def run_final(scale, both):
    def body(*refs):
        final_kernel(scale, *refs)

    whole = VMEM((C, 3 * C), F32)
    out = array((C, 3 * C), F32)
    cost = (1_000_000, 2_000_000)
    return call(body, (), (both,), (), out, [whole, dma((4,))], cost, out_away=True)


def shards(frames_in, cotangent, counts, norm_gain, norm_shift, spatial_weight, temporal_weight):
    shape = frames_in.shape
    x = frames_in.reshape(ROWS, C)
    g = cotangent.reshape(ROWS, C)
    place = lax.axis_index("tm").astype(jnp.int32).reshape(1)
    core = lax.axis_index("c").astype(jnp.int32).reshape(1)
    w_t = spatial_weight.T
    wt_t = temporal_weight.T
    tm_size = lax.axis_size("tm")
    pairs = [[], []]
    for c in range(2):
        for t in range(tm_size - 1):
            here = c * tm_size + t
            pairs[(t + c) % 2] += [(here, here + 1), (here + 1, here)]

    one, two, g_own = run_edge(place, core, counts, g)
    one = lax.ppermute(one, ("c", "tm"), pairs[0])
    two = lax.ppermute(two, ("c", "tm"), pairs[1])
    y, u, whole, last, stats, wt_own, x_own = run_forward(
        place, g_own, counts, x, norm_gain, norm_shift, wt_t, w_t
    )
    keep, send = run_grad(place, core, whole, u, last, one, two)

    near, far = groups()
    size = len(near[0])
    part = run_add(core, keep, lax.all_gather(send, "c")).reshape(size, HALF // size, LANES)
    part = run_sum(exchange(part, near), len(far[0]))
    part, one = lax.optimization_barrier((part, one))
    d_in = run_backward(
        place, core, y, g_own, one, two, wt_own, stats, x_own, counts, norm_gain, norm_shift, w_t
    )
    part, d_in = lax.optimization_barrier((exchange(part, far), d_in))
    part = run_sum(part, size)
    mine = exchange(part, near).reshape(HALF, LANES)
    both = lax.all_gather(mine, "c")

    frames = lax.axis_size(("z", "c")) * 2 * tm_size
    grad = run_final(1.0 / math.sqrt(frames * HH * WW), both)
    return (d_in.reshape(shape), grad.T)


def groups():
    zs, ys, xs = lax.axis_size("z"), lax.axis_size("tm") // X_SIZE, X_SIZE

    def at(z, c, y, x):
        return ((z * 2 + c) * ys + y) * xs + x

    def kind(i):
        return bin(i).count("1") % 2

    def pair(i):
        return sorted((i, i + 1), key=kind)

    def alike(i, size):
        return [p for p in range(size) if kind(p) == i]

    near = [
        [at(zz, c, yy, x ^ (x >> 1)) for x in range(xs) for zz in pair(z) for yy in pair(y)]
        for z in range(0, zs, 2)
        for c in range(2)
        for y in range(0, ys, 2)
    ]
    far = [
        [at(z, c, y, x) for z in alike(i, zs) for y in alike(j, ys)]
        for i in range(2)
        for j in range(2)
        for c in range(2)
        for x in range(xs)
    ]
    return near, far


def exchange(parts, members):
    return lax.all_to_all(parts, ("z", "c", "tm"), 0, 0, axis_index_groups=members, tiled=True)


def solution(mesh):
    devices = mesh.devices
    dp, tm = devices.shape
    split = Mesh(devices.reshape(dp // 2, 2, tm), ("z", "c", "tm"))
    return jax.shard_map(
        shards,
        mesh=split,
        in_specs=(
            P(("z", "c"), "tm", None, None, None),
            P(("z", "c"), "tm", None, None, None),
            P(("z", "c"), None),
            P(),
            P(),
            P(),
            P(),
        ),
        out_specs=(P(("z", "c"), "tm", None, None, None), P()),
        check_vma=False,
    )
```

```python
import math

import jax
import jax.numpy as jnp
from jax import lax
from jax.experimental import pallas as pl
from jax.experimental.pallas import tpu as pltpu
from jax.sharding import Mesh
from jax.sharding import PartitionSpec as P

F32 = jnp.float32
BF16 = jnp.bfloat16
C = 320
GROUPS = 32
PER_GROUP = C // GROUPS
CAP = 3
HH = 32
WW = 8
PIX = HH * WW
ROWS = CAP * PIX
ENTRIES = PIX * PER_GROUP
VMEM = pltpu.VMEM
LANES = 128
X_SIZE = 4
HALF = 4 * C
PARAMS = pltpu.CompilerParams(vmem_limit_bytes=28 * 1024 * 1024)


def group_matrix():
    row = lax.broadcasted_iota(jnp.int32, (C, C), 0).astype(F32)
    col = lax.broadcasted_iota(jnp.int32, (C, C), 1).astype(F32)
    inv = 1.0 / PER_GROUP
    same = jnp.floor((row + 0.5) * inv) == jnp.floor((col + 0.5) * inv)
    return same.astype(F32).astype(BF16)


def group_mean(sums, matrix):
    high = sums.astype(BF16).astype(F32)
    rest = sums - high
    middle = rest.astype(BF16).astype(F32)
    terms = jnp.concatenate([high, middle, rest - middle, jnp.zeros((8, C), F32)], axis=0)
    added = jnp.dot(terms.astype(BF16), matrix, preferred_element_type=F32)
    return (added[0:8] + added[8:16] + added[16:24]) / ENTRIES


def frame(s):
    if isinstance(s, int):
        return pl.ds(s * PIX, PIX)
    return pl.ds(pl.multiple_of(s * PIX, PIX), PIX)


def sigmoid(values):
    return 0.5 * jnp.tanh(0.5 * values) + 0.5


def shifted(values, step):
    cube = values.reshape(HH, WW, C)
    rolled = jnp.roll(cube, -step, axis=1)
    col = lax.broadcasted_iota(jnp.int32, (HH, WW, C), 1)
    keep = (col < WW - 1) if step > 0 else (col > 0)
    return jnp.where(keep, rolled, 0.0).reshape(PIX, C)


def down(values):
    return jnp.concatenate([jnp.zeros((WW, C), F32), values[:-WW]], axis=0)


def up(values):
    return jnp.concatenate([values[WW:], jnp.zeros((WW, C), F32)], axis=0)


def start_all(sems, *pairs):
    copies = [pltpu.make_async_copy(src, dst, sems.at[i]) for i, (src, dst) in enumerate(pairs)]
    for copy in copies:
        copy.start()
    return copies


def packed(values):
    half = PIX // 2
    rest = values[:, 2 * LANES :]
    rest = jnp.concatenate([rest[:half], rest[half:]], axis=1)
    return jnp.concatenate([values[:, :LANES], values[:, LANES : 2 * LANES], rest], axis=0)


def unpacked(values):
    rest = values[2 * PIX :, :]
    tail = C - 2 * LANES
    rest = jnp.concatenate([rest[:, :tail], rest[:, tail:]], axis=0)
    return jnp.concatenate([values[:PIX], values[PIX : 2 * PIX], rest], axis=1)


def left_first(t_ref, core_ref):
    return lax.rem(t_ref[0] + core_ref[0], 2)


def edge_kernel(
    t_ref, core_ref, counts_hbm, g_hbm, one_ref, two_ref, g_ref, counts, sems
):
    frames = [(g_hbm.at[frame(s), :], g_ref.at[frame(s), :]) for s in range(CAP)]
    for copy in start_all(sems, (counts_hbm, counts), *frames):
        copy.wait()
    last = counts[0, t_ref[0]] - 1
    turn = left_first(t_ref, core_ref)
    one_ref[...] = packed(g_ref[frame(last * (1 - turn)), :])
    two_ref[...] = packed(g_ref[frame(last * turn), :])


def forward_kernel(
    t_ref, g_ref, counts_hbm, x_hbm, gain_hbm, shift_hbm, wt_hbm, w_hbm, y_ref, u_ref, whole_ref,
    last_ref, stats_ref, wt_ref, x_ref, inner, flipped, counts, gain_ref, shift_ref, w_ref, cols, wst, prod, sems,
):
    weights = [(w_hbm.at[pl.ds(q, 80), :], w_ref.at[pl.ds(q, 80), :]) for q in range(0, C, 80)]
    frames = [(x_hbm.at[frame(s), :], x_ref.at[frame(s), :]) for s in range(CAP)]
    copies = start_all(
        sems,
        *frames,
        (gain_hbm, gain_ref),
        (shift_hbm, shift_ref),
        (counts_hbm, counts),
        *weights,
        (wt_hbm, wt_ref),
    )
    matrix = group_matrix()
    blank = jnp.zeros((8 - CAP, C), F32)

    def per_frame(fn):
        return jnp.concatenate([fn(s) for s in range(CAP)] + [blank], axis=0)

    flipped[...] = g_ref[...].T
    edge = 3 * C - 3 * C % LANES
    whole_ref[:, edge:] = jnp.zeros((C, 8 * LANES - edge), F32)
    for copy in copies[:CAP]:
        copy.wait()

    def load(s):
        return x_ref[s * PIX : (s + 1) * PIX, :].astype(F32)

    mean = group_mean(per_frame(lambda s: jnp.sum(load(s), axis=0, keepdims=True)), matrix)

    def squares(s):
        centred = load(s) - mean[s : s + 1]
        return jnp.sum(centred * centred, axis=0, keepdims=True)

    inv = lax.rsqrt(group_mean(per_frame(squares), matrix) + 1e-05)
    stats_ref[0] = mean
    stats_ref[1] = inv
    for copy in copies[CAP : CAP + 3]:
        copy.wait()
    n = counts[0, t_ref[0]]
    gain = gain_ref[...].reshape(1, C)
    shift = shift_ref[...].reshape(1, C)

    def activate(s):
        values = (x_ref[frame(s), :].astype(F32) - stats_ref[0, pl.ds(s, 1), :]) * stats_ref[
            1, pl.ds(s, 1), :
        ] * gain + shift
        act = values * sigmoid(values)
        cols[frame(s), 0:C] = shifted(act, -1).astype(BF16)
        cols[frame(s), C : 2 * C] = act.astype(BF16)
        cols[frame(s), 2 * C : 3 * C] = shifted(act, 1).astype(BF16)

    for s in range(CAP):
        activate(s)
    for copy in copies[CAP + 3 : -1]:
        copy.wait()
    for i in range(3):
        wst[i * C : (i + 1) * C, :] = w_ref[:, i * 3 * C : (i + 1) * 3 * C]
    prod[...] = lax.dot_general(
        cols[...], wst[...], (((1,), (1,)), ((), ())), preferred_element_type=F32
    )

    zero = jnp.zeros((PIX, C), BF16)

    def add(s):
        rows = frame(s)
        mixed = down(prod[rows, 0:C]) + prod[rows, C : 2 * C] + up(prod[rows, 2 * C : 3 * C])
        y = (x_ref[rows, :].astype(F32) + mixed).astype(BF16)
        y_ref[rows, :] = y
        yf = y.astype(F32)
        units = (yf * sigmoid(yf)).astype(BF16)
        u_ref[rows, :] = jnp.where(jnp.int32(s) < n, units, zero)
        if s < CAP - 1:
            inner[rows, :] = jnp.where(jnp.int32(s + 1) < n, units, zero)

    for s in range(CAP):
        add(s)
    last_ref[...] = u_ref[frame(n - 1), :]

    def term(own, taken):
        return jnp.dot(own, taken, preferred_element_type=F32)

    whole_ref[:, 0:C] = term(flipped[:, PIX:], inner[...])
    whole_ref[:, C : 2 * C] = term(flipped[...], u_ref[...])
    whole_ref[:, 2 * C : 3 * C] = term(flipped[:, 0 : ROWS - PIX], u_ref[PIX:, :])
    copies[-1].wait()


def sides(turn, one_ref, two_ref):
    before = jnp.where(turn == 1, one_ref[...], two_ref[...])
    after = jnp.where(turn == 1, two_ref[...], one_ref[...])
    return unpacked(before), unpacked(after)


def grad_kernel(
    t_ref, core_ref, whole_ref, u_ref, last_ref, one_ref, two_ref, keep_ref, send_ref, whole
):
    core = core_ref[0]
    before, after = sides(left_first(t_ref, core_ref), one_ref, two_ref)
    whole[...] = whole_ref[...]
    whole[:, 0:C] += jnp.dot(after.T, last_ref[...], preferred_element_type=F32)
    whole[:, 2 * C : 3 * C] += jnp.dot(before.T, u_ref[0:PIX, :], preferred_element_type=F32)
    for j in range(4):
        first = whole[:, j * LANES : (j + 1) * LANES]
        second = whole[:, (j + 4) * LANES : (j + 5) * LANES]
        keep_ref[j * C : (j + 1) * C, :] = jnp.where(core == 0, first, second)
        send_ref[j * C : (j + 1) * C, :] = jnp.where(core == 0, second, first).astype(BF16)


def backward_kernel(
    t_ref, core_ref, y_ref, g_ref, one_ref, two_ref, wt_ref, stats_ref, x_ref, counts_hbm, gain_hbm,
    shift_hbm, w_hbm, out_ref, ext, dys, counts, gain_ref, shift_ref, w_ref, cols, wst, prod, sems,
):
    weights = [(w_hbm.at[pl.ds(q, 80), :], w_ref.at[pl.ds(q, 80), :]) for q in range(0, C, 80)]
    copies = start_all(
        sems,
        (counts_hbm, counts),
        *weights,
        (gain_hbm, gain_ref),
        (shift_hbm, shift_ref),
    )
    before, after = sides(left_first(t_ref, core_ref), one_ref, two_ref)
    ext[0:PIX, :] = before
    ext[PIX : PIX + ROWS, :] = g_ref[...]
    ext[PIX + ROWS :, :] = after
    copies[0].wait()
    n = counts[0, t_ref[0]]
    ext[frame(n + 1), :] = after
    for s in range(CAP):
        back = jnp.zeros((PIX, C), F32)
        for k in range(3):
            back = back + jnp.dot(
                ext[frame(s + 2 - k), :],
                wt_ref[:, k * C : (k + 1) * C],
                preferred_element_type=F32,
            )
        yf = y_ref[frame(s), :].astype(F32)
        sig = sigmoid(yf)
        back = (sig * (1.0 + yf * (1.0 - sig)) * back).astype(BF16)
        dy = (g_ref[frame(s), :].astype(F32) + back.astype(F32)).astype(BF16)
        dys[frame(s), :] = dy
        dyf = dy.astype(F32)
        cols[frame(s), 0:C] = shifted(dyf, 1).astype(BF16)
        cols[frame(s), C : 2 * C] = dy
        cols[frame(s), 2 * C : 3 * C] = shifted(dyf, -1).astype(BF16)
    for copy in copies[1:]:
        copy.wait()
    for i in range(3):
        for j in range(3):
            tap = 3 * i + j
            wst[j * C : (j + 1) * C, i * C : (i + 1) * C] = w_ref[:, tap * C : (tap + 1) * C]
    prod[...] = jnp.dot(cols[...], wst[...], preferred_element_type=F32)
    matrix = group_matrix()
    gain = gain_ref[...].reshape(1, C)
    shift = shift_ref[...].reshape(1, C)

    def finish(s):
        rows = frame(s)
        da = up(prod[rows, 0:C]) + prod[rows, C : 2 * C] + down(prod[rows, 2 * C : 3 * C])
        mean = stats_ref[0, pl.ds(s, 1), :]
        inv = stats_ref[1, pl.ds(s, 1), :]
        normed = (x_ref[rows, :].astype(F32) - mean) * inv
        values = normed * gain + shift
        sig = sigmoid(values)
        dn = da * (sig * (1.0 + values * (1.0 - sig))) * gain
        sums = jnp.concatenate(
            [
                jnp.sum(dn, axis=0, keepdims=True),
                jnp.sum(dn * normed, axis=0, keepdims=True),
                jnp.zeros((6, C), F32),
            ],
            axis=0,
        )
        means = group_mean(sums, matrix)
        dx = inv * (dn - means[0:1] - normed * means[1:2])
        total = dys[rows, :].astype(F32) + dx
        out_ref[rows, :] = jnp.where(jnp.int32(s) < n, total, 0.0).astype(BF16)

    for s in range(CAP):
        finish(s)


def add_kernel(core_ref, keep_ref, both_ref, out_ref):
    got = jnp.where(core_ref[0] == 0, both_ref[1], both_ref[0])
    out_ref[...] = (keep_ref[...] + got.astype(F32)).astype(BF16)


def sum_kernel(copies, x_ref, out_ref):
    total = x_ref[0].astype(F32)
    for i in range(1, x_ref.shape[0]):
        total = total + x_ref[i].astype(F32)
    total = total.astype(BF16)
    for i in range(copies):
        out_ref[i] = total


def final_kernel(scale, both_ref, out_hbm, whole, sems):
    copies = []
    for i, row in enumerate(range(0, C, C // 4)):
        rows = pl.ds(row, C // 4)
        for j in range(8):
            width = min(LANES, 3 * C - j * LANES)
            start = (j % 4) * C + row
            part = both_ref[j // 4, start : start + C // 4, :].astype(F32) * scale
            whole[rows, j * LANES : j * LANES + width] = part[:, :width]
        copies.append(pltpu.make_async_copy(whole.at[rows, :], out_hbm.at[rows, :], sems.at[i]))
        copies[-1].start()
    for copy in copies:
        copy.wait()


SMEM_SPEC = pl.BlockSpec(memory_space=pltpu.SMEM)
VMEM_SPEC = pl.BlockSpec(memory_space=pltpu.VMEM)
HBM_SPEC = pl.BlockSpec(memory_space=pltpu.HBM)


def call(body, scalars, arrays, away, outs, scratch, cost, out_away=False):
    away = [pltpu.with_memory_space_constraint(a, pltpu.HBM) for a in away]
    out_spec = HBM_SPEC if out_away else VMEM_SPEC
    return pl.pallas_call(
        body,
        out_shape=outs,
        in_specs=[SMEM_SPEC] * len(scalars) + [VMEM_SPEC] * len(arrays) + [HBM_SPEC] * len(away),
        out_specs=[VMEM_SPEC] * len(outs) if isinstance(outs, list) else out_spec,
        scratch_shapes=scratch,
        compiler_params=PARAMS,
        cost_estimate=pl.CostEstimate(flops=cost[0], bytes_accessed=cost[1], transcendentals=0),
    )(*scalars, *arrays, *away)


array = jax.ShapeDtypeStruct
dma = pltpu.SemaphoreType.DMA
ACT = array((ROWS, C), BF16)
ONE = array((PIX * C // LANES, LANES), BF16)
VECTOR = VMEM((C,), F32)
WEIGHTS = VMEM((C, 9 * C), BF16)
COLUMNS = VMEM((ROWS, 3 * C), BF16)
STACKED = VMEM((3 * C, 3 * C), BF16)
PRODUCT = VMEM((ROWS, 3 * C), F32)


def counts_mem(counts):
    return pltpu.SMEM(counts.shape, jnp.int32)


def run_edge(place, core, counts, g):
    return call(
        edge_kernel,
        (place, core),
        (),
        (counts, g),
        [ONE, ONE, ACT],
        [counts_mem(counts), dma((4,))],
        (0, 600_000),
    )


def run_forward(place, g_own, counts, x, gain, shift, wt_t, w_t):
    return call(
        forward_kernel,
        (place,),
        (g_own,),
        (counts, x, gain, shift, wt_t, w_t),
        [
            ACT, ACT, array((C, 8 * LANES), F32), array((PIX, C), BF16), array((2, 8, C), F32),
            array(wt_t.shape, BF16), ACT,
        ],
        [
            VMEM((ROWS - PIX, C), BF16), VMEM((C, ROWS), BF16), counts_mem(counts), VECTOR, VECTOR,
            WEIGHTS, COLUMNS, STACKED, PRODUCT, dma((11,)),
        ],
        (2 * ROWS * 12 * C * C, 4_000_000),
    )


def run_grad(place, core, whole, u, last, one, two):
    return call(
        grad_kernel,
        (place, core),
        (whole, u, last, one, two),
        (),
        [array((HALF, LANES), F32), array((HALF, LANES), BF16)],
        [VMEM((C, 8 * LANES), F32)],
        (4 * PIX * C * C, 2_500_000),
    )


def run_backward(place, core, y, g_own, one, two, wt_own, stats, x_own, counts, gain, shift, w_t):
    return call(
        backward_kernel,
        (place, core),
        (y, g_own, one, two, wt_own, stats, x_own),
        (counts, gain, shift, w_t),
        ACT,
        [
            VMEM((5 * PIX, C), BF16), VMEM((ROWS, C), BF16), counts_mem(counts), VECTOR, VECTOR,
            WEIGHTS, COLUMNS, STACKED, PRODUCT, dma((7,)),
        ],
        (2 * ROWS * 12 * C * C, 4_000_000),
    )


def run_sum(parts, copies):
    def body(*refs):
        sum_kernel(copies, *refs)

    out = array((copies,) + parts.shape[1:], BF16)
    return call(body, (), (parts,), (), out, [], (parts.size, 2 * parts.size))


def run_add(core, keep, both):
    out = array(keep.shape, BF16)
    return call(add_kernel, (core,), (keep, both), (), out, [], (keep.size, 8 * keep.size))


def run_final(scale, both):
    def body(*refs):
        final_kernel(scale, *refs)

    whole = VMEM((C, 3 * C), F32)
    out = array((C, 3 * C), F32)
    cost = (1_000_000, 2_000_000)
    return call(body, (), (both,), (), out, [whole, dma((4,))], cost, out_away=True)


def shards(frames_in, cotangent, counts, norm_gain, norm_shift, spatial_weight, temporal_weight):
    shape = frames_in.shape
    x = frames_in.reshape(ROWS, C)
    g = cotangent.reshape(ROWS, C)
    place = lax.axis_index("tm").astype(jnp.int32).reshape(1)
    core = lax.axis_index("c").astype(jnp.int32).reshape(1)
    w_t = spatial_weight.T
    wt_t = temporal_weight.T
    tm_size = lax.axis_size("tm")
    pairs = [[], []]
    for c in range(2):
        for t in range(tm_size - 1):
            here = c * tm_size + t
            pairs[(t + c) % 2] += [(here, here + 1), (here + 1, here)]

    one, two, g_own = run_edge(place, core, counts, g)
    one = lax.ppermute(one, ("c", "tm"), pairs[0])
    two = lax.ppermute(two, ("c", "tm"), pairs[1])
    y, u, whole, last, stats, wt_own, x_own = run_forward(
        place, g_own, counts, x, norm_gain, norm_shift, wt_t, w_t
    )
    keep, send = run_grad(place, core, whole, u, last, one, two)

    near, far = groups()
    size = len(near[0])
    part = run_add(core, keep, lax.all_gather(send, "c")).reshape(size, HALF // size, LANES)
    part = run_sum(exchange(part, near), len(far[0]))
    part, one = lax.optimization_barrier((part, one))
    d_in = run_backward(
        place, core, y, g_own, one, two, wt_own, stats, x_own, counts, norm_gain, norm_shift, w_t
    )
    part, d_in = lax.optimization_barrier((exchange(part, far), d_in))
    part = run_sum(part, size)
    mine = exchange(part, near).reshape(HALF, LANES)
    both = lax.all_gather(mine, "c")

    frames = lax.axis_size(("z", "c")) * 2 * tm_size
    grad = run_final(1.0 / math.sqrt(frames * HH * WW), both)
    return (d_in.reshape(shape), grad.T)


def groups():
    zs, ys, xs = lax.axis_size("z"), lax.axis_size("tm") // X_SIZE, X_SIZE

    def at(z, c, y, x):
        return ((z * 2 + c) * ys + y) * xs + x

    def kind(i):
        return bin(i).count("1") % 2

    def pair(i):
        return sorted((i, i + 1), key=kind)

    def alike(i, size):
        return [p for p in range(size) if kind(p) == i]

    near = [
        [at(pair(z)[k // 2], c, pair(y)[(k ^ (k >> 1)) % 2], x ^ (x >> 1)) for x in range(xs) for k in range(4)]
        for z in range(0, zs, 2)
        for c in range(2)
        for y in range(0, ys, 2)
    ]
    far = [
        [at(z, c, y, x) for z in alike(i, zs) for y in alike(j, ys)]
        for i in range(2)
        for j in range(2)
        for c in range(2)
        for x in range(xs)
    ]
    return near, far


def exchange(parts, members):
    return lax.all_to_all(parts, ("z", "c", "tm"), 0, 0, axis_index_groups=members, tiled=True)


def solution(mesh):
    devices = mesh.devices
    dp, tm = devices.shape
    split = Mesh(devices.reshape(dp // 2, 2, tm), ("z", "c", "tm"))
    return jax.shard_map(
        shards,
        mesh=split,
        in_specs=(
            P(("z", "c"), "tm", None, None, None),
            P(("z", "c"), "tm", None, None, None),
            P(("z", "c"), None),
            P(),
            P(),
            P(),
            P(),
        ),
        out_specs=(P(("z", "c"), "tm", None, None, None), P()),
        check_vma=False,
    )
```
